256 devices in a mesh: gx: 16 (over x_lo, z), gy: 8 (over y, core), gz: 2 (over x_hi).
Axes of the slice: x: 4 (x_hi: 2, x_lo: 2; x = x_hi * 2 + x_lo), y: 4, z: 8, core: 2. Of those that a mesh axis runs over, the one named last changes fastest.
Arguments:
- section_fields: float32 [25, 16, 512, 1024], P(None, 'gz', 'gx', 'gy'), may hold values from -4 to 4
- base_fields: float32 [25, 16, 512, 1024], P(None, 'gz', 'gx', 'gy'), may hold values from -6 to 6
- flags: int32 [16, 8], P('gx', 'gy'), may hold values 0 or 1
Outputs:
- next_fields: float32 [25, 16, 512, 1024], P(None, 'gz', 'gx', 'gy')
The draws below stay inside these ranges and needn't reach their ends.
All inputs are finite; a program needn't handle non-finite values. No bound on the sum of `flags` on one device may be relied on, other than what follows from the above.
Results may differ from the reference program's by a relative error of at most 0.0001.
Values sent between devices are 32-bit elements; how exact they have to be, the bound alone decides.
A program may use at most 128 MiB of HBM per device.

```python
import jax
import jax.numpy as jnp
from jax import lax

FIELDS = 25
BX = 32
BY = 128
NX = 512
NY = 1024
NZ = 16
BLOCKS_X = 16
BLOCKS_Y = 8


def set_ends(values, rng, smallest, high):
    index_at = [jax.random.randint(jax.random.fold_in(rng, axis), (), 0, length) for axis, length in enumerate(values.shape)]
    longest = values.shape.index(max(values.shape))
    neighbour = index_at[:longest] + [(index_at[longest] + 1) % values.shape[longest]] + index_at[longest + 1:]
    return values.at[tuple(index_at)].set(smallest).at[tuple(neighbour)].set(high)


def block_scale(own_key, extent, cuts, low, top_value):
    level, own = 1.0, jax.random.fold_in(own_key, 6)
    for position, parts in cuts:
        heights = jnp.exp(jax.random.uniform(jax.random.fold_in(own, position), (parts,), jnp.float32, low / len(cuts), top_value / len(cuts)))
        level = level * jnp.repeat(heights, extent[position] // parts).reshape([-1 if axis == position else 1 for axis in range(len(extent))])
    return level


def centred(stream_key, shape, deviation, reach, shards=(), held_as=jnp.bfloat16):
    gain = block_scale(stream_key, shape, shards, -0.22, 0.18) if shards else 1.0
    result = jax.random.normal(stream_key, shape, jnp.float32) * deviation * gain
    return jnp.minimum(jnp.maximum(result, -reach), reach).astype(held_as)


def setup_inputs(seed: int = 0) -> dict:
    keys = jax.random.split(jax.random.key(seed), 4)
    return {
        "section_fields": centred(keys[0], (FIELDS, NZ, NX, NY), 0.5, 4.0, ((1, 2), (2, 16), (3, 8)), jnp.float32),
        "base_fields": centred(keys[1], (FIELDS, NZ, NX, NY), 1.0, 6.0, ((1, 2), (2, 16), (3, 8)), jnp.float32),
        "flags": set_ends((jax.random.randint(keys[2], (BLOCKS_X, BLOCKS_Y), 0, 4) < 1).astype(jnp.int32), jax.random.fold_in(keys[2], 1), 0, 1),
    }


PAIRS = ((0, 0), (0, 1), (0, 2), (1, 1), (1, 2), (2, 2))
SIGN_TABLE = (1.0, 1.0, 1.0, -1.0, 1.0, -1.0, 1.0, 1.0, 1.0, 1.0, -1.0, 1.0, -1.0, 1.0, -1.0, -1.0, 1.0, 1.0, 1.0, -1.0, -1.0, 1.0, -1.0, -1.0, 1.0)


def sym_index(i, j):
    return PAIRS.index((min(i, j), max(i, j)))


def differences(padded, axis, count):
    def shifted(k):
        return lax.slice_in_dim(padded, 3 + k, 3 + k + count, axis=axis)
    centre = shifted(0)
    first = (shifted(-2) - 8.0 * shifted(-1) + 8.0 * shifted(1) - shifted(2)) / 12.0
    second = (-shifted(-2) + 16.0 * shifted(-1) - 30.0 * centre + 16.0 * shifted(1) - shifted(2)) / 12.0
    smooth = (shifted(-3) + shifted(3) - 6.0 * (shifted(-2) + shifted(2)) + 15.0 * (shifted(-1) + shifted(1)) - 20.0 * centre) / 64.0
    return first, second, smooth


def evolve(state, first, second, smooth, sigma):
    conformal = state[0]
    trace_k = state[7]
    lapse = state[17]
    theta = state[18]

    def metric(i, j):
        return state[1 + sym_index(i, j)]

    def curv(i, j):
        return state[8 + sym_index(i, j)]

    def grad_shift(k, j):
        return first[j][19 + k]

    div = grad_shift(0, 0) + grad_shift(1, 1) + grad_shift(2, 2)
    lap = second[0][17] + second[1][17] + second[2][17]
    square = sum(curv(i, j) * curv(i, j) for i in range(3) for j in range(3))
    rhs_chi = (2.0 / 3.0) * conformal * (lapse * trace_k - div)
    rhs_metric = []
    rhs_curv = []
    for (i, j) in PAIRS:
        lie_g = sum(metric(i, k) * grad_shift(k, j) + metric(j, k) * grad_shift(k, i) for k in range(3))
        rhs_metric.append(-2.0 * lapse * curv(i, j) + lie_g - (2.0 / 3.0) * metric(i, j) * div)
        lie_a = sum(curv(i, k) * grad_shift(k, j) + curv(j, k) * grad_shift(k, i) for k in range(3))
        quad = sum(curv(i, k) * curv(k, j) for k in range(3))
        term = lapse * (trace_k * curv(i, j) - 2.0 * quad) + lie_a - (2.0 / 3.0) * curv(i, j) * div
        if i == j:
            term = term + conformal * (lap / 3.0 - second[i][17])
        rhs_curv.append(term)
    rhs_k = -conformal * lap + lapse * (square + trace_k * trace_k / 3.0)
    rhs_gamma = []
    for i in range(3):
        value = second[0][19 + i] + second[1][19 + i] + second[2][19 + i]
        value = value - 2.0 * sum(curv(i, j) * first[j][17] for j in range(3))
        value = value + (2.0 / 3.0) * state[14 + i] * div
        value = value - sum(state[14 + j] * grad_shift(i, j) for j in range(3))
        rhs_gamma.append(value)
    rhs_lapse = -2.0 * lapse * (trace_k - 2.0 * theta)
    rhs_theta = lapse * (trace_k * trace_k / 3.0 - 0.5 * square) - 0.04 * lapse * theta
    rhs_shift = [0.75 * state[22 + i] for i in range(3)]
    rhs_driver = [rhs_gamma[i] - 2.0 * state[22 + i] for i in range(3)]
    pieces = [rhs_chi] + rhs_metric + [rhs_k] + rhs_curv + rhs_gamma + [rhs_lapse, rhs_theta] + rhs_shift + rhs_driver
    rhs = jnp.stack(pieces, axis=0)
    advect = state[19][None] * first[0] + state[20][None] * first[1] + state[21][None] * first[2]
    return rhs + advect + sigma * smooth


def edge_copy(block, axis, start):
    edge = lax.slice_in_dim(block, start, start + 1, axis=axis)
    return jnp.concatenate([edge, edge, edge], axis=axis)


def reference(section_fields, base_fields, flags):
    section = section_fields
    count_z, count_x, count_y = section.shape[1], section.shape[2], section.shape[3]
    signs = jnp.array(SIGN_TABLE, dtype=jnp.float32)[:, None, None, None]
    padded_z = jnp.concatenate([section[:, count_z - 3:], section, section[:, :3]], axis=1)
    ghost_low = section[:, :, 2::-1, ::-1] * signs
    padded_x = jnp.concatenate([ghost_low, section, edge_copy(section, 2, count_x - 1)], axis=2)
    padded_y = jnp.concatenate([edge_copy(section, 3, 0), section, edge_copy(section, 3, count_y - 1)], axis=3)
    diff_z = differences(padded_z, 1, count_z)
    diff_x = differences(padded_x, 2, count_x)
    diff_y = differences(padded_y, 3, count_y)
    first = (diff_x[0], diff_y[0], diff_z[0])
    second = (diff_x[1], diff_y[1], diff_z[1])
    smooth = diff_x[2] + diff_y[2] + diff_z[2]
    flag_cells = jnp.repeat(jnp.repeat(flags.astype(jnp.float32), BX, axis=0), BY, axis=1)
    sigma = (0.05 + 0.75 * flag_cells)[None, None]
    rhs = evolve(section, first, second, smooth, sigma)
    return base_fields + 0.25 * rhs
```

```python
import jax
import jax.numpy as jnp
from jax import lax
from jax.experimental import pallas as pl
from jax.experimental.pallas import tpu as pltpu
from jax.sharding import PartitionSpec as P

MESH = pl.DeviceIdType.MESH
FIELDS = 25
PAIRS = ((0, 0), (0, 1), (0, 2), (1, 1), (1, 2), (2, 2))
NEGATIVE = (3, 5, 10, 12, 14, 15, 19, 20, 22, 23)
FIRST = (17, 19, 20, 21)
REST = FIELDS - len(FIRST)
ROWS_Z, ROWS_X, ROWS_Y = 8, 32, 128
TILES = ROWS_X // 8
STEP = 0.25


def rest_field(p):
    return jnp.where(p < 17, p, jnp.where(p < 18, 18, p + 4))


def places():
    gx, gy, gz = lax.axis_index("gx"), lax.axis_index("gy"), lax.axis_index("gz")
    low = gx // 8
    across = (1 - low) * 8 + gx % 8
    plus = (across, gy, jnp.where(low == 1, 1 - gz, gz))
    minus = (across, gy, jnp.where(low == 0, 1 - gz, gz))
    partner = (gx, gy, 1 - gz)
    left = (gx, (gy + 7) % 8, gz)
    right = (gx, (gy + 1) % 8, gz)
    below = (jnp.where(gx == 0, 0, gx - 1), jnp.where(gx == 0, 7 - gy, gy), gz)
    above = (gx + 1, gy, gz)
    return gx, gy, plus, minus, partner, left, right, below, above


def remote(src, dst, send, recv, device):
    return pltpu.make_async_remote_copy(
        src_ref=src, dst_ref=dst, send_sem=send, recv_sem=recv, device_id=device, device_id_type=MESH
    )


def sym(i, j):
    return PAIRS.index((min(i, j), max(i, j)))


def evolve(s, d, dd):
    chi, trace, lapse, theta = s[0], s[7], s[17], s[18]
    g = lambda i, j: s[1 + sym(i, j)]
    a = lambda i, j: s[8 + sym(i, j)]
    grad = lambda k, j: d[19 + k][j]
    div = grad(0, 0) + grad(1, 1) + grad(2, 2)
    lap = dd[17][0] + dd[17][1] + dd[17][2]
    div23 = (2.0 / 3.0) * div
    square = (
        a(0, 0) * a(0, 0) + a(1, 1) * a(1, 1) + a(2, 2) * a(2, 2)
        + 2.0 * (a(0, 1) * a(0, 1) + a(0, 2) * a(0, 2) + a(1, 2) * a(1, 2))
    )
    out = {}
    out[0] = chi * ((2.0 / 3.0) * (lapse * trace) - div23)
    lapse2 = 2.0 * lapse
    for n, (i, j) in enumerate(PAIRS):
        if i == j:
            lie_g = 2.0 * sum(g(i, k) * grad(k, i) for k in range(3))
            lie_a = 2.0 * sum(a(i, k) * grad(k, i) for k in range(3))
        else:
            lie_g = sum(g(i, k) * grad(k, j) + g(j, k) * grad(k, i) for k in range(3))
            lie_a = sum(a(i, k) * grad(k, j) + a(j, k) * grad(k, i) for k in range(3))
        out[1 + n] = lie_g - lapse2 * a(i, j) - g(i, j) * div23
        quad = sum(a(i, k) * a(k, j) for k in range(3))
        term = lapse * (trace * a(i, j)) - lapse2 * quad + lie_a - a(i, j) * div23
        if i == j:
            term = term + chi * (lap * (1.0 / 3.0) - dd[17][i])
        out[8 + n] = term
    third = trace * trace * (1.0 / 3.0)
    out[7] = lapse * (square + third) - chi * lap
    for i in range(3):
        value = dd[19 + i][0] + dd[19 + i][1] + dd[19 + i][2]
        value = value - 2.0 * sum(a(i, j) * d[17][j] for j in range(3))
        value = value + s[14 + i] * div23
        value = value - sum(s[14 + j] * grad(i, j) for j in range(3))
        out[14 + i] = value
        out[22 + i] = value - 2.0 * s[22 + i]
        out[19 + i] = 0.75 * s[22 + i]
    out[17] = -lapse2 * (trace - 2.0 * theta)
    out[18] = lapse * (third - 0.5 * square) - 0.04 * (lapse * theta)
    return out


def kernel(
    sec, base, flag, signs, out,
    pad, acc, relay_p, relay_m, packed, from_left, from_right,
    load_sem, store_sem, z_send, z_recv, x_send, x_recv, y_send, y_recv,
):
    gx, gy, plus, minus, partner, left, right, below, above = places()
    inner = (slice(3, 11), slice(8, 40))
    load_s = pltpu.make_async_copy(sec, pad.at[:, 3:11, 8:40, :], load_sem.at[0])
    load_b = pltpu.make_async_copy(base, acc, load_sem.at[1])
    load_s.start()
    load_b.start()

    barrier = pltpu.get_barrier_semaphore()
    for device in (plus, minus, partner, left, right, below):
        pl.semaphore_signal(barrier, inc=1, device_id=device, device_id_type=MESH)

    @pl.when(gx < 15)
    def _():
        pl.semaphore_signal(barrier, inc=1, device_id=above, device_id_type=MESH)
        pl.semaphore_wait(barrier, 7)

    @pl.when(gx == 15)
    def _():
        pl.semaphore_wait(barrier, 6)

    def direct(n, f):
        return (
            remote(sec.at[f, 0:3], pad.at[f, 11:14, 8:40, :], z_send.at[0, n], z_recv.at[0, n], partner),
            remote(sec.at[f, 5:8], pad.at[f, 0:3, 8:40, :], z_send.at[1, n], z_recv.at[1, n], partner),
        )

    def hop1(p):
        f, n = rest_field(p), p + len(FIRST)
        return (
            remote(sec.at[f, 0:3], relay_p.at[p], z_send.at[0, n], z_recv.at[0, n], plus),
            remote(sec.at[f, 5:8], relay_m.at[p], z_send.at[1, n], z_recv.at[1, n], minus),
        )

    def hop2(p):
        f, n = rest_field(p), p + len(FIRST)
        return (
            remote(relay_p.at[p], pad.at[f, 11:14, 8:40, :], z_send.at[2, n], z_recv.at[2, n], plus),
            remote(relay_m.at[p], pad.at[f, 0:3, 8:40, :], z_send.at[3, n], z_recv.at[3, n], minus),
        )

    for n, f in enumerate(FIRST):
        for copy in direct(n, f):
            copy.start()

    to_above = remote(sec.at[:, :, 29:32, :], pad.at[:, 3:11, 5:8, :], x_send.at[3], x_recv.at[3], above)
    to_below = remote(sec.at[:, :, 0:3, :], pad.at[:, 3:11, 40:43, :], x_send.at[4], x_recv.at[4], below)
    to_mirror = [
        remote(sec.at[:, :, i:i + 1, :], pad.at[:, 3:11, 7 - i:8 - i, :], x_send.at[i], x_recv.at[i], below)
        for i in range(3)
    ]

    @pl.when(gx < 15)
    def _():
        to_above.start()

    @pl.when(gx > 0)
    def _():
        to_below.start()

    @pl.when(gx == 0)
    def _():
        for copy in to_mirror:
            copy.start()

    @pl.loop(0, REST)
    def _(p):
        for copy in hop1(p):
            copy.start()

    lane = lax.broadcasted_iota(jnp.int32, (8, 128), 1)
    load_s.wait()

    @pl.loop(0, ROWS_Z * TILES)
    def _(i):
        z, row = i // TILES, pl.multiple_of((i % TILES) * 8, 8)
        both = [jnp.zeros((8, 128), jnp.float32) for _ in range(2)]
        for f in range(FIELDS):
            half, slot = divmod(f, 16)
            tile = pltpu.roll(pad[f, z + 3, pl.ds(row + 8, 8), :], 3 + 8 * slot, 1)
            both[half] = jnp.where(lane >= 8 * slot, tile, both[half])
        for half in range(2):
            packed[half, z, pl.ds(row, 8), :] = both[half]

    to_left = remote(packed, from_right, y_send.at[0], y_recv.at[0], left)
    to_right = remote(packed, from_left, y_send.at[1], y_recv.at[1], right)
    to_left.start()
    to_right.start()

    @pl.when(gx > 0)
    def _():
        to_above.wait_recv()

    @pl.when(gx < 15)
    def _():
        to_below.wait_recv()

    @pl.when(gx == 0)
    def _():
        for copy in to_mirror:
            copy.wait_recv()
        turn = jnp.where(
            lax.broadcasted_iota(jnp.int32, (128, 128), 0) + lax.broadcasted_iota(jnp.int32, (128, 128), 1) == 127,
            1.0, 0.0,
        )

        @pl.loop(0, FIELDS)
        def _(f):
            rows = pad[f, 3:11, 0:8, :].reshape(64, 128)
            rows = jnp.dot(rows, turn, precision=lax.Precision.HIGHEST, preferred_element_type=jnp.float32)
            pad[f, 3:11, 0:8, :] = (rows * signs[f]).reshape(8, 8, 128)

    @pl.when(gx == 15)
    def _():
        @pl.loop(0, FIELDS)
        def _(f):
            edge = pad[f, 3:11, 39:40, :]
            pad[f, 3:11, 40:43, :] = jnp.broadcast_to(edge, (8, 3, 128))

    to_right.wait_recv()
    to_left.wait_recv()
    place = lane % 8

    @pl.loop(0, ROWS_Z * TILES)
    def _(i):
        z, row = i // TILES, pl.multiple_of((i % TILES) * 8, 8)
        for half in range(2):
            at = (half, z, pl.ds(row, 8), slice(None))
            own = packed[at]
            low = jnp.where(
                place == 0, pltpu.roll(own, 125, 1),
                jnp.where(place == 1, pltpu.roll(own, 126, 1), pltpu.roll(own, 127, 1)),
            )
            high = jnp.where(
                place == 3, pltpu.roll(own, 1, 1),
                jnp.where(place == 4, pltpu.roll(own, 2, 1), pltpu.roll(own, 3, 1)),
            )
            low = jnp.where(gy == 0, low, from_left[at])
            high = jnp.where(gy == 7, high, from_right[at])
            from_left[at] = jnp.where(place < 3, low, high)

    load_b.wait()
    for n, f in enumerate(FIRST):
        for copy in direct(n, f):
            copy.wait_recv()

    sigma = 0.05 + 0.75 * flag[0, 0].astype(jnp.float32)
    damp = sigma * (STEP / 64.0)

    @pl.loop(0, ROWS_Z * TILES)
    def _(i):
        z, row = i // TILES, pl.multiple_of((i % TILES) * 8, 8)

        @pl.when(i < REST)
        def _():
            for copy in hop1(i):
                copy.wait_recv()
            for copy in hop2(i):
                copy.start()

        here = (z + 3, pl.ds(row + 8, 8), slice(None))
        ghosts = [from_left[half, z, pl.ds(row, 8), :] for half in range(2)]
        s = [pad[(f,) + here] for f in range(FIELDS)]
        d, dd = {}, {}
        bx, by = s[19] * (STEP / 12.0), s[20] * (STEP / 12.0)
        partial = {}
        for f in FIRST + tuple(f for f in range(FIELDS) if f not in FIRST):
            c = s[f]
            half, slot = divmod(f, 16)
            ghost = pltpu.roll(ghosts[half], (128 - 8 * slot - 3) % 128, 1)
            up = [pad[f, z + 3, pl.ds(row + 8 + k, 8), :] for k in (1, 2, 3)]
            down = [pad[f, z + 3, pl.ds(row + 8 - k, 8), :] for k in (1, 2, 3)]
            right_ = [pltpu.roll(jnp.where(lane < k, ghost, c), 128 - k, 1) for k in (1, 2, 3)]
            left_ = [pltpu.roll(jnp.where(lane >= 128 - k, ghost, c), k, 1) for k in (1, 2, 3)]
            dx = 8.0 * (up[0] - down[0]) - (up[1] - down[1])
            dy = 8.0 * (right_[0] - left_[0]) - (right_[1] - left_[1])
            sx = [up[k] + down[k] for k in range(3)]
            sy = [right_[k] + left_[k] for k in range(3)]
            smooth = (sx[2] + sy[2]) - 6.0 * (sx[1] + sy[1]) + 15.0 * (sx[0] + sy[0]) - 40.0 * c
            partial[f] = bx * dx + by * dy + damp * smooth
            if f in FIRST:
                zs = {k: pad[f, z + 3 + k, pl.ds(row + 8, 8), :] for k in (-2, -1, 1, 2)}
                dz = 8.0 * (zs[1] - zs[-1]) - (zs[2] - zs[-2])
                sz = [zs[1] + zs[-1], zs[2] + zs[-2]]
                d[f] = [v * (1.0 / 12.0) for v in (dx, dy, dz)]
                dd[f] = [(16.0 * v[0] - v[1] - 30.0 * c) * (1.0 / 12.0) for v in (sx, sy, sz)]
        rhs = evolve(s, d, dd)
        for f in range(FIELDS):
            at = (f, z, pl.ds(row, 8), slice(None))
            acc[at] = acc[at] + (partial[f] + STEP * rhs[f])

    def along_z(f):
        @pl.loop(0, TILES)
        def _(t):
            row = pl.multiple_of(t * 8, 8)
            v = [pad[f, z, pl.ds(row + 8, 8), :] for z in range(14)]
            for z in range(8):
                w = v[z:z + 7]
                bz = pad[21, z + 3, pl.ds(row + 8, 8), :] * (STEP / 12.0)
                dz = 8.0 * (w[4] - w[2]) - (w[5] - w[1])
                smooth = (w[6] + w[0]) - 6.0 * (w[5] + w[1]) + 15.0 * (w[4] + w[2]) - 20.0 * w[3]
                at = (f, z, pl.ds(row, 8), slice(None))
                acc[at] = acc[at] + (bz * dz + damp * smooth)

    def store(f):
        return pltpu.make_async_copy(acc.at[f], out.at[f], store_sem.at[f])

    for f in FIRST:
        along_z(f)
        store(f).start()

    @pl.loop(0, REST)
    def _(p):
        f = rest_field(p)
        for copy in hop2(p):
            copy.wait_recv()
        along_z(f)
        store(f).start()

    for n, f in enumerate(FIRST):
        for copy in direct(n, f):
            copy.wait_send()

    @pl.loop(0, REST)
    def _(p):
        for copy in hop1(p):
            copy.wait_send()
        for copy in hop2(p):
            copy.wait_send()

    @pl.when(gx < 15)
    def _():
        to_above.wait_send()

    @pl.when(gx > 0)
    def _():
        to_below.wait_send()

    @pl.when(gx == 0)
    def _():
        for copy in to_mirror:
            copy.wait_send()

    to_left.wait_send()
    to_right.wait_send()

    @pl.loop(0, FIELDS)
    def _(f):
        store(f).wait()


def body(section_fields, base_fields, flags):
    f32 = jnp.float32
    signs = jnp.array([-1.0 if c in NEGATIVE else 1.0 for c in range(FIELDS)], f32)
    block = (FIELDS, ROWS_Z, ROWS_X, ROWS_Y)
    dma = pltpu.SemaphoreType.DMA
    return pl.pallas_call(
        kernel,
        out_shape=jax.ShapeDtypeStruct(block, f32),
        in_specs=[
            pl.BlockSpec(memory_space=pl.ANY),
            pl.BlockSpec(memory_space=pl.ANY),
            pl.BlockSpec(memory_space=pltpu.SMEM),
            pl.BlockSpec(memory_space=pltpu.SMEM),
        ],
        out_specs=pl.BlockSpec(memory_space=pl.ANY),
        scratch_shapes=[
            pltpu.VMEM((FIELDS, 14, 48, ROWS_Y), f32),
            pltpu.VMEM(block, f32),
            pltpu.VMEM((REST, 3, ROWS_X, ROWS_Y), f32),
            pltpu.VMEM((REST, 3, ROWS_X, ROWS_Y), f32),
            pltpu.VMEM((2, ROWS_Z, ROWS_X, ROWS_Y), f32),
            pltpu.VMEM((2, ROWS_Z, ROWS_X, ROWS_Y), f32),
            pltpu.VMEM((2, ROWS_Z, ROWS_X, ROWS_Y), f32),
            dma((2,)),
            dma((FIELDS,)),
            dma((4, FIELDS)),
            dma((4, FIELDS)),
            dma((5,)),
            dma((5,)),
            dma((2,)),
            dma((2,)),
        ],
        compiler_params=pltpu.CompilerParams(
            collective_id=0, has_side_effects=True, vmem_limit_bytes=48 * 2**20
        ),
        cost_estimate=pl.CostEstimate(flops=80_000_000, bytes_accessed=9_830_400, transcendentals=0),
        name="substep",
    )(section_fields, base_fields, flags, signs)


def solution(mesh):
    spec = P(None, "gz", "gx", "gy")
    return jax.shard_map(
        body, mesh=mesh, in_specs=(spec, spec, P("gx", "gy")), out_specs=spec, check_vma=False
    )
```

```python
import jax
import jax.numpy as jnp
from jax import lax
from jax.experimental import pallas as pl
from jax.experimental.pallas import tpu as pltpu
from jax.sharding import PartitionSpec as P

MESH = pl.DeviceIdType.MESH
FIELDS = 25
PAIRS = ((0, 0), (0, 1), (0, 2), (1, 1), (1, 2), (2, 2))
NEGATIVE = (3, 5, 10, 12, 14, 15, 19, 20, 22, 23)
NEGATIVE_BITS = sum(1 << c for c in NEGATIVE)
FIRST = (17, 19, 20, 21)
EARLY = 8
ROWS_Z, ROWS_X, ROWS_Y = 8, 32, 128
TILES = ROWS_X // 8
STEP = 0.25


def field_at(n):
    rest = jnp.where(n < 21, n - 4, jnp.where(n < 22, 18, n))
    return jnp.where(n < 1, 17, jnp.where(n < 4, 18 + n, rest))


def remote(src, dst, send, recv, device):
    return pltpu.make_async_remote_copy(
        src_ref=src, dst_ref=dst, send_sem=send, recv_sem=recv, device_id=device, device_id_type=MESH
    )


def sym(i, j):
    return PAIRS.index((min(i, j), max(i, j)))


def evolve(s, d, dd):
    chi, trace, lapse, theta = s[0], s[7], s[17], s[18]
    g = lambda i, j: s[1 + sym(i, j)]
    a = lambda i, j: s[8 + sym(i, j)]
    grad = lambda k, j: d[19 + k][j]
    div = grad(0, 0) + grad(1, 1) + grad(2, 2)
    lap = dd[17][0] + dd[17][1] + dd[17][2]
    div23 = (2.0 / 3.0) * div
    square = (
        a(0, 0) * a(0, 0) + a(1, 1) * a(1, 1) + a(2, 2) * a(2, 2)
        + 2.0 * (a(0, 1) * a(0, 1) + a(0, 2) * a(0, 2) + a(1, 2) * a(1, 2))
    )
    out = {}
    out[0] = chi * ((2.0 / 3.0) * (lapse * trace) - div23)
    lapse2 = 2.0 * lapse
    for n, (i, j) in enumerate(PAIRS):
        if i == j:
            lie_g = 2.0 * sum(g(i, k) * grad(k, i) for k in range(3))
            lie_a = 2.0 * sum(a(i, k) * grad(k, i) for k in range(3))
        else:
            lie_g = sum(g(i, k) * grad(k, j) + g(j, k) * grad(k, i) for k in range(3))
            lie_a = sum(a(i, k) * grad(k, j) + a(j, k) * grad(k, i) for k in range(3))
        out[1 + n] = lie_g - lapse2 * a(i, j) - g(i, j) * div23
        quad = sum(a(i, k) * a(k, j) for k in range(3))
        term = lapse * (trace * a(i, j)) - lapse2 * quad + lie_a - a(i, j) * div23
        if i == j:
            term = term + chi * (lap * (1.0 / 3.0) - dd[17][i])
        out[8 + n] = term
    third = trace * trace * (1.0 / 3.0)
    out[7] = lapse * (square + third) - chi * lap
    for i in range(3):
        value = dd[19 + i][0] + dd[19 + i][1] + dd[19 + i][2]
        value = value - 2.0 * sum(a(i, j) * d[17][j] for j in range(3))
        value = value + s[14 + i] * div23
        value = value - sum(s[14 + j] * grad(i, j) for j in range(3))
        out[14 + i] = value
        out[22 + i] = value - 2.0 * s[22 + i]
        out[19 + i] = 0.75 * s[22 + i]
    out[17] = -lapse2 * (trace - 2.0 * theta)
    out[18] = lapse * (third - 0.5 * square) - 0.04 * (lapse * theta)
    return out


def kernel(
    sec, base, flag, out,
    pad, acc, cross, packed, from_left, from_right, flag_at,
    load_sem, store_sem, z_send, z_recv, x_send, x_recv, y_send, y_recv, leg_send, leg_recv, arrive_recv, hello,
):
    gx, gy, gz = lax.axis_index("gx"), lax.axis_index("gy"), lax.axis_index("gz")
    low, z, core = gx // 8, gx % 8, gy % 2
    partner = (gx, gy, 1 - gz)
    left, right = (gx, (gy + 7) % 8, gz), (gx, (gy + 1) % 8, gz)
    up, down = (gx + 1, gy, gz), (gx - 1, gy, gz)
    mirror = (0, 7 - gy, gz)
    last, first = (7, gy, gz), (8, gy, gz)
    is_last, is_first = gx == 7, gx == 8
    in_row = lambda half, q: (8 * half + q, gy, gz)

    load_s = pltpu.make_async_copy(sec, pad.at[:, 3:11, 8:40, :], load_sem.at[0])
    load_b = pltpu.make_async_copy(base, acc, load_sem.at[1])
    load_f = pltpu.make_async_copy(flag, flag_at, load_sem.at[2])
    load_s.start()
    load_b.start()
    load_f.start()

    barrier = pltpu.get_barrier_semaphore()

    def tell(semaphore, device):
        pl.semaphore_signal(semaphore, inc=1, device_id=device, device_id_type=MESH)

    tell(barrier, partner)

    @pl.when(core == 1)
    def _():
        tell(barrier, left)
        tell(barrier, right)

    @pl.when((core == 1) & (gx == 0))
    def _():
        tell(barrier, mirror)

    @pl.when(z < 7)
    def _():
        tell(barrier, up)

    @pl.when(gx != 7)
    def _():
        tell(barrier, last)

    @pl.when(is_first)
    def _():
        for q in range(8):
            tell(barrier, in_row(0, q))
            if q > 0:
                tell(barrier, in_row(1, q))

    expected = (
        1 + jnp.where(core == 0, 2, 0) + jnp.where((core == 0) & (gx == 0), 1, 0) + jnp.where(z > 0, 1, 0)
        + jnp.where(is_last, 15, 0) + jnp.where(is_first, 0, 1)
    )
    pl.semaphore_wait(barrier, expected)

    def z_copies(n):
        f = field_at(n)
        return (
            remote(sec.at[f, 0:3], pad.at[f, 11:14, 8:40, :], z_send.at[0, n], z_recv.at[0, n], partner),
            remote(sec.at[f, 5:8], pad.at[f, 0:3, 8:40, :], z_send.at[1, n], z_recv.at[1, n], partner),
        )

    @pl.loop(0, EARLY)
    def _(n):
        for copy in z_copies(n):
            copy.start()

    @pl.when(z > 0)
    def _():
        tell(hello.at[0], down)

    @pl.when(core == 0)
    def _():
        tell(hello.at[1], left)
        tell(hello.at[1], right)

    @pl.when((core == 0) & (gx == 0))
    def _():
        tell(hello.at[2], mirror)

    @pl.when(low == 0)
    def _():
        tell(hello.at[3], first)

    @pl.when(is_last)
    def _():
        for q in range(7):
            tell(hello.at[4], in_row(0, q))

    to_up = remote(sec.at[:, :, 29:32, :], pad.at[:, 3:11, 5:8, :], x_send.at[3], x_recv.at[3], up)
    to_down = remote(sec.at[:, :, 0:3, :], pad.at[:, 3:11, 40:43, :], x_send.at[4], x_recv.at[4], down)
    to_mirror = [
        remote(sec.at[:, :, i:i + 1, :], pad.at[:, 3:11, 7 - i:8 - i, :], x_send.at[i], x_recv.at[i], mirror)
        for i in range(3)
    ]

    def leg_out(half, q):
        rows = slice(29, 32) if half == 0 else slice(0, 3)
        own = q == 7 * half
        ghost = piece_ghost(half, q) if own else cross.at[:, 0:3, :]
        return remote(
            sec.at[:, q, rows, :], ghost, leg_send.at[q], arrive_recv.at[q] if own else leg_recv.at[0], in_row(1 - half, q)
        )

    def piece_ghost(half, q):
        return pad.at[:, 3 + q, 5:8, :] if half == 0 else pad.at[:, 3 + q, 40:43, :]

    def leg_in(half):
        return remote(
            cross.at[:, 0:3, :], piece_ghost(half, z), leg_send.at[8], arrive_recv.at[z], first if half == 0 else last
        )

    def piece(half, q):
        return remote(cross.at[:, 0:3, :], piece_ghost(half, q), leg_send.at[8], arrive_recv.at[q], first)

    @pl.when(z > 0)
    def _():
        to_down.start()

    @pl.when(is_last)
    def _():
        for q in range(8):
            leg_out(0, q).start()

    lane = lax.broadcasted_iota(jnp.int32, (8, 128), 1)
    load_s.wait()

    @pl.loop(0, ROWS_Z * TILES)
    def _(i):
        z, row = i // TILES, pl.multiple_of((i % TILES) * 8, 8)
        both = [jnp.zeros((8, 128), jnp.float32) for _ in range(2)]
        for f in range(FIELDS):
            half, slot = divmod(f, 16)
            tile = pltpu.roll(pad[f, z + 3, pl.ds(row + 8, 8), :], 3 + 8 * slot, 1)
            both[half] = jnp.where(lane >= 8 * slot, tile, both[half])
        for half in range(2):
            packed[half, z, pl.ds(row, 8), :] = both[half]

    to_left = remote(packed, from_right, y_send.at[0], y_recv.at[0], left)
    to_right = remote(packed, from_left, y_send.at[1], y_recv.at[1], right)

    @pl.when(core == 1)
    def _():
        pl.semaphore_wait(hello.at[1], 2)

    @pl.when(gy > 0)
    def _():
        to_left.start()

    @pl.when(gy < 7)
    def _():
        to_right.start()

    @pl.when(z < 7)
    def _():
        pl.semaphore_wait(hello.at[0], 1)
        to_up.start()

    @pl.when((core == 1) & (gx == 0))
    def _():
        pl.semaphore_wait(hello.at[2], 1)

    @pl.when(gx == 0)
    def _():
        for copy in to_mirror:
            copy.start()

    @pl.when(is_first)
    def _():
        pl.semaphore_wait(hello.at[3], 8)
        for q in range(8):
            leg_out(1, q).start()

    @pl.loop(EARLY, FIELDS)
    def _(n):
        for copy in z_copies(n):
            copy.start()

    @pl.when(gx < 7)
    def _():
        pl.semaphore_wait(hello.at[4], 1)
        leg_out(1, 0).wait_recv()
        leg_in(1).start()

    @pl.when(gx > 8)
    def _():
        leg_out(0, 1).wait_recv()
        leg_in(0).start()

    place = lax.broadcasted_iota(jnp.int32, (ROWS_X, 128), 1) % 8

    @pl.when(gy > 0)
    def _():
        to_right.wait_recv()

    @pl.when(gy < 7)
    def _():
        to_left.wait_recv()

    @pl.when(gy == 0)
    def _():
        @pl.loop(0, 2 * ROWS_Z)
        def _(i):
            own = packed[i // ROWS_Z, i % ROWS_Z]
            from_left[i // ROWS_Z, i % ROWS_Z] = jnp.where(
                place == 0, pltpu.roll(own, 125, 1),
                jnp.where(place == 1, pltpu.roll(own, 126, 1), pltpu.roll(own, 127, 1)),
            )

    @pl.when(gy == 7)
    def _():
        @pl.loop(0, 2 * ROWS_Z)
        def _(i):
            own = packed[i // ROWS_Z, i % ROWS_Z]
            from_right[i // ROWS_Z, i % ROWS_Z] = jnp.where(
                place == 3, pltpu.roll(own, 1, 1),
                jnp.where(place == 4, pltpu.roll(own, 2, 1), pltpu.roll(own, 3, 1)),
            )

    load_b.wait()
    load_f.wait()
    for n in range(len(FIRST)):
        for copy in z_copies(n):
            copy.wait_recv()

    sigma = 0.05 + 0.75 * flag_at[0, 0].astype(jnp.float32)
    damp = sigma * (STEP / 64.0)

    def tile(z, row):
        here = (z + 3, pl.ds(row + 8, 8), slice(None))
        ghosts = [
            jnp.where(lane % 8 < 3, from_left[half, z, pl.ds(row, 8), :], from_right[half, z, pl.ds(row, 8), :])
            for half in range(2)
        ]
        s = [pad[(f,) + here] for f in range(FIELDS)]
        d, dd = {}, {}
        bx, by = s[19] * (STEP / 12.0), s[20] * (STEP / 12.0)
        partial = {}
        for f in FIRST + tuple(f for f in range(FIELDS) if f not in FIRST):
            c = s[f]
            half, slot = divmod(f, 16)
            ghost = pltpu.roll(ghosts[half], (128 - 8 * slot - 3) % 128, 1)
            up = [pad[f, z + 3, pl.ds(row + 8 + k, 8), :] for k in (1, 2, 3)]
            down = [pad[f, z + 3, pl.ds(row + 8 - k, 8), :] for k in (1, 2, 3)]
            right_ = [pltpu.roll(jnp.where(lane < k, ghost, c), 128 - k, 1) for k in (1, 2, 3)]
            left_ = [pltpu.roll(jnp.where(lane >= 128 - k, ghost, c), k, 1) for k in (1, 2, 3)]
            dx = 8.0 * (up[0] - down[0]) - (up[1] - down[1])
            dy = 8.0 * (right_[0] - left_[0]) - (right_[1] - left_[1])
            sx = [up[k] + down[k] for k in range(3)]
            sy = [right_[k] + left_[k] for k in range(3)]
            smooth = (sx[2] + sy[2]) - 6.0 * (sx[1] + sy[1]) + 15.0 * (sx[0] + sy[0]) - 40.0 * c
            partial[f] = bx * dx + by * dy + damp * smooth
            if f in FIRST:
                zs = {k: pad[f, z + 3 + k, pl.ds(row + 8, 8), :] for k in (-2, -1, 1, 2)}
                dz = 8.0 * (zs[1] - zs[-1]) - (zs[2] - zs[-2])
                sz = [zs[1] + zs[-1], zs[2] + zs[-2]]
                d[f] = [v * (1.0 / 12.0) for v in (dx, dy, dz)]
                dd[f] = [(16.0 * v[0] - v[1] - 30.0 * c) * (1.0 / 12.0) for v in (sx, sy, sz)]
        rhs = evolve(s, d, dd)
        for f in range(FIELDS):
            at = (f, z, pl.ds(row, 8), slice(None))
            acc[at] = acc[at] + (partial[f] + STEP * rhs[f])

    @pl.loop(0, 2 * ROWS_Z)
    def _(i):
        tile(i // 2, pl.multiple_of(8 + 8 * (i % 2), 8))

    @pl.when(z > 0)
    def _():
        to_up.wait_recv()

    @pl.when(z < 7)
    def _():
        to_down.wait_recv()

    @pl.when(is_first)
    def _():
        for q in range(8):
            piece(0, q).wait_recv()

    @pl.when(is_last)
    def _():
        for q in range(8):
            piece(1, q).wait_recv()

    @pl.when(gx == 0)
    def _():
        for copy in to_mirror:
            copy.wait_recv()
        turn = jnp.where(
            lax.broadcasted_iota(jnp.int32, (128, 128), 0) + lax.broadcasted_iota(jnp.int32, (128, 128), 1) == 127,
            1.0, 0.0,
        )

        @pl.loop(0, FIELDS)
        def _(f):
            sign = (1 - 2 * ((NEGATIVE_BITS >> f) & 1)).astype(jnp.float32)
            rows = pad[f, 3:11, 0:8, :].reshape(64, 128)
            rows = jnp.dot(rows, turn, precision=lax.Precision.HIGHEST, preferred_element_type=jnp.float32)
            pad[f, 3:11, 0:8, :] = (rows * sign).reshape(8, 8, 128)

    @pl.when(gx == 15)
    def _():
        @pl.loop(0, FIELDS)
        def _(f):
            edge = pad[f, 3:11, 39:40, :]
            pad[f, 3:11, 40:43, :] = jnp.broadcast_to(edge, (8, 3, 128))

    @pl.loop(0, 2 * ROWS_Z)
    def _(i):
        tile(i // 2, pl.multiple_of(24 * (i % 2), 8))

    def along_z(f):
        @pl.loop(0, TILES)
        def _(t):
            row = pl.multiple_of(t * 8, 8)
            v = [pad[f, z, pl.ds(row + 8, 8), :] for z in range(14)]
            for z in range(8):
                w = v[z:z + 7]
                bz = pad[21, z + 3, pl.ds(row + 8, 8), :] * (STEP / 12.0)
                dz = 8.0 * (w[4] - w[2]) - (w[5] - w[1])
                smooth = (w[6] + w[0]) - 6.0 * (w[5] + w[1]) + 15.0 * (w[4] + w[2]) - 20.0 * w[3]
                at = (f, z, pl.ds(row, 8), slice(None))
                acc[at] = acc[at] + (bz * dz + damp * smooth)

    def store(f):
        return pltpu.make_async_copy(acc.at[f], out.at[f], store_sem.at[f])

    @pl.loop(0, FIELDS)
    def _(n):
        @pl.when(n >= len(FIRST))
        def _():
            for copy in z_copies(n):
                copy.wait_recv()

        f = field_at(n)
        along_z(f)
        store(f).start()

    @pl.loop(0, FIELDS)
    def _(n):
        for copy in z_copies(n):
            copy.wait_send()

    @pl.when(z > 0)
    def _():
        to_down.wait_send()

    @pl.when(z < 7)
    def _():
        to_up.wait_send()

    @pl.when(gx == 0)
    def _():
        for copy in to_mirror:
            copy.wait_send()

    @pl.when(is_last)
    def _():
        for q in range(8):
            leg_out(0, q).wait_send()

    @pl.when(is_first)
    def _():
        for q in range(8):
            leg_out(1, q).wait_send()

    @pl.when((gx != 7) & (gx != 8))
    def _():
        piece(0, 0).wait_send()

    @pl.when(gy > 0)
    def _():
        to_left.wait_send()

    @pl.when(gy < 7)
    def _():
        to_right.wait_send()

    @pl.loop(0, FIELDS)
    def _(f):
        store(f).wait()


def body(section_fields, base_fields, flags):
    f32 = jnp.float32
    block = (FIELDS, ROWS_Z, ROWS_X, ROWS_Y)
    dma = pltpu.SemaphoreType.DMA
    return pl.pallas_call(
        kernel,
        out_shape=jax.ShapeDtypeStruct(block, f32),
        in_specs=[
            pl.BlockSpec(memory_space=pl.ANY),
            pl.BlockSpec(memory_space=pl.ANY),
            pl.BlockSpec(memory_space=pl.ANY),
        ],
        out_specs=pl.BlockSpec(memory_space=pl.ANY),
        scratch_shapes=[
            pltpu.VMEM((FIELDS, 14, 48, ROWS_Y), f32),
            pltpu.VMEM(block, f32),
            pltpu.VMEM((FIELDS, 8, ROWS_Y), f32),
            pltpu.VMEM((2, ROWS_Z, ROWS_X, ROWS_Y), f32),
            pltpu.VMEM((2, ROWS_Z, ROWS_X, ROWS_Y), f32),
            pltpu.VMEM((2, ROWS_Z, ROWS_X, ROWS_Y), f32),
            pltpu.SMEM((1, 1), jnp.int32),
            dma((3,)),
            dma((FIELDS,)),
            dma((2, FIELDS)),
            dma((2, FIELDS)),
            dma((5,)),
            dma((5,)),
            dma((2,)),
            dma((2,)),
            dma((9,)),
            dma((1,)),
            dma((8,)),
            pltpu.SemaphoreType.REGULAR((5,)),
        ],
        compiler_params=pltpu.CompilerParams(
            collective_id=0, has_side_effects=True, vmem_limit_bytes=48 * 2**20
        ),
        cost_estimate=pl.CostEstimate(flops=80_000_000, bytes_accessed=9_830_400, transcendentals=0),
        name="substep",
    )(section_fields, base_fields, flags)


def solution(mesh):
    spec = P(None, "gz", "gx", "gy")
    return jax.shard_map(
        body, mesh=mesh, in_specs=(spec, spec, P("gx", "gy")), out_specs=spec, check_vma=False
    )
```

```python
import jax
import jax.numpy as jnp
from jax import lax
from jax.experimental import pallas as pl
from jax.experimental.pallas import tpu as pltpu
from jax.sharding import PartitionSpec as P

MESH = pl.DeviceIdType.MESH
FIELDS = 25
PAIRS = ((0, 0), (0, 1), (0, 2), (1, 1), (1, 2), (2, 2))
NEGATIVE = (3, 5, 10, 12, 14, 15, 19, 20, 22, 23)
NEGATIVE_BITS = sum(1 << c for c in NEGATIVE)
FIRST = (17, 19, 20, 21)
EARLY = 8
NEAR = 2
ROWS_Z, ROWS_X, ROWS_Y = 8, 32, 128
TILES = ROWS_X // 8
STEP = 0.25


def field_at(n):
    rest = jnp.where(n < 21, n - 4, jnp.where(n < 22, 18, n))
    return jnp.where(n < 1, 17, jnp.where(n < 4, 18 + n, rest))


def remote(src, dst, send, recv, device):
    return pltpu.make_async_remote_copy(
        src_ref=src, dst_ref=dst, send_sem=send, recv_sem=recv, device_id=device, device_id_type=MESH
    )


def sym(i, j):
    return PAIRS.index((min(i, j), max(i, j)))


def evolve(s, d, dd):
    chi, trace, lapse, theta = s[0], s[7], s[17], s[18]
    g = lambda i, j: s[1 + sym(i, j)]
    a = lambda i, j: s[8 + sym(i, j)]
    grad = lambda k, j: d[19 + k][j]
    div = grad(0, 0) + grad(1, 1) + grad(2, 2)
    lap = dd[17][0] + dd[17][1] + dd[17][2]
    div23 = (2.0 / 3.0) * div
    square = (
        a(0, 0) * a(0, 0) + a(1, 1) * a(1, 1) + a(2, 2) * a(2, 2)
        + 2.0 * (a(0, 1) * a(0, 1) + a(0, 2) * a(0, 2) + a(1, 2) * a(1, 2))
    )
    out = {}
    out[0] = chi * ((2.0 / 3.0) * (lapse * trace) - div23)
    lapse2 = 2.0 * lapse
    for n, (i, j) in enumerate(PAIRS):
        if i == j:
            lie_g = 2.0 * sum(g(i, k) * grad(k, i) for k in range(3))
            lie_a = 2.0 * sum(a(i, k) * grad(k, i) for k in range(3))
        else:
            lie_g = sum(g(i, k) * grad(k, j) + g(j, k) * grad(k, i) for k in range(3))
            lie_a = sum(a(i, k) * grad(k, j) + a(j, k) * grad(k, i) for k in range(3))
        out[1 + n] = lie_g - lapse2 * a(i, j) - g(i, j) * div23
        quad = sum(a(i, k) * a(k, j) for k in range(3))
        term = lapse * (trace * a(i, j)) - lapse2 * quad + lie_a - a(i, j) * div23
        if i == j:
            term = term + chi * (lap * (1.0 / 3.0) - dd[17][i])
        out[8 + n] = term
    third = trace * trace * (1.0 / 3.0)
    out[7] = lapse * (square + third) - chi * lap
    for i in range(3):
        value = dd[19 + i][0] + dd[19 + i][1] + dd[19 + i][2]
        value = value - 2.0 * sum(a(i, j) * d[17][j] for j in range(3))
        value = value + s[14 + i] * div23
        value = value - sum(s[14 + j] * grad(i, j) for j in range(3))
        out[14 + i] = value
        out[22 + i] = value - 2.0 * s[22 + i]
        out[19 + i] = 0.75 * s[22 + i]
    out[17] = -lapse2 * (trace - 2.0 * theta)
    out[18] = lapse * (third - 0.5 * square) - 0.04 * (lapse * theta)
    return out


def kernel(
    sec, base, flag, acc,
    pad, cross, packed, from_left, from_right, flag_at,
    load_sem, z_send, z_recv, x_send, x_recv, y_send, y_recv, leg_send, leg_recv, arrive_recv, hello,
):
    gx, gy, gz = lax.axis_index("gx"), lax.axis_index("gy"), lax.axis_index("gz")
    low, z, core = gx // 8, gx % 8, gy % 2
    partner = (gx, gy, 1 - gz)
    left, right = (gx, (gy + 7) % 8, gz), (gx, (gy + 1) % 8, gz)
    up, down = (gx + 1, gy, gz), (gx - 1, gy, gz)
    mirror = (0, 7 - gy, gz)
    last, first = (7, gy, gz), (8, gy, gz)
    is_last, is_first = gx == 7, gx == 8
    in_row = lambda half, q: (8 * half + q, gy, gz)

    load_s = pltpu.make_async_copy(sec, pad.at[:, 3:11, 8:40, :], load_sem.at[0])
    load_b = pltpu.make_async_copy(base, acc, load_sem.at[1])
    load_f = pltpu.make_async_copy(flag, flag_at, load_sem.at[2])
    barrier = pltpu.get_barrier_semaphore()

    def tell(semaphore, device):
        pl.semaphore_signal(semaphore, inc=1, device_id=device, device_id_type=MESH)

    tell(barrier, partner)
    load_s.start()
    load_b.start()
    load_f.start()

    @pl.when(core == 1)
    def _():
        tell(barrier, left)
        tell(barrier, right)

    @pl.when((core == 1) & (gx == 0))
    def _():
        tell(barrier, mirror)

    @pl.when(z < 7)
    def _():
        tell(barrier, up)

    @pl.when(z < NEAR)
    def _():
        tell(barrier, last)

    @pl.when(gx == 0)
    def _():
        tell(barrier, first)

    @pl.when(is_first)
    def _():
        for q in range(8):
            if q > 0:
                tell(barrier, in_row(0, q))
                tell(barrier, in_row(1, q))

    expected = (
        1 + jnp.where(core == 0, 2, 0) + jnp.where((core == 0) & (gx == 0), 1, 0) + jnp.where(z > 0, 1, 0)
        + jnp.where(is_last, 2 * NEAR, 0) + jnp.where(gx == 0, 0, 1)
    )
    pl.semaphore_wait(barrier, expected)

    def z_copies(n):
        f = field_at(n)
        return (
            remote(sec.at[f, 0:3], pad.at[f, 11:14, 8:40, :], z_send.at[0, n], z_recv.at[0, n], partner),
            remote(sec.at[f, 5:8], pad.at[f, 0:3, 8:40, :], z_send.at[1, n], z_recv.at[1, n], partner),
        )

    @pl.loop(0, EARLY)
    def _(n):
        for copy in z_copies(n):
            copy.start()

    @pl.when(z > 0)
    def _():
        tell(hello.at[0], down)

    @pl.when(core == 0)
    def _():
        tell(hello.at[1], left)
        tell(hello.at[1], right)

    @pl.when((core == 0) & (gx == 0))
    def _():
        tell(hello.at[2], mirror)

    @pl.when(((low == 0) & (z > 0)) | (z >= NEAR))
    def _():
        tell(hello.at[3], first)

    @pl.when(is_last)
    def _():
        for q in range(NEAR):
            tell(hello.at[4], in_row(0, q))
        tell(hello.at[5], first)

    to_up = remote(sec.at[:, :, 29:32, :], pad.at[:, 3:11, 5:8, :], x_send.at[3], x_recv.at[3], up)
    to_down = remote(sec.at[:, :, 0:3, :], pad.at[:, 3:11, 40:43, :], x_send.at[4], x_recv.at[4], down)
    to_mirror = [
        remote(sec.at[:, :, i:i + 1, :], pad.at[:, 3:11, 7 - i:8 - i, :], x_send.at[i], x_recv.at[i], mirror)
        for i in range(3)
    ]

    def leg_out(half, q):
        rows = slice(29, 32) if half == 0 else slice(0, 3)
        own = q == 7 * half
        ghost = piece_ghost(half, q) if own else cross.at[:, 0:3, :]
        return remote(
            sec.at[:, q, rows, :], ghost, leg_send.at[q], arrive_recv.at[q] if own else leg_recv.at[0], in_row(1 - half, q)
        )

    def piece_ghost(half, q):
        return pad.at[:, 3 + q, 5:8, :] if half == 0 else pad.at[:, 3 + q, 40:43, :]

    def leg_in(half):
        return remote(
            cross.at[:, 0:3, :], piece_ghost(half, z), leg_send.at[8], arrive_recv.at[z], first if half == 0 else last
        )

    def piece(half, q):
        return remote(cross.at[:, 0:3, :], piece_ghost(half, q), leg_send.at[8], arrive_recv.at[q], first)

    @pl.when(z > 0)
    def _():
        to_down.start()

    @pl.when(is_last)
    def _():
        for q in range(NEAR):
            leg_out(0, q).start()

    lane = lax.broadcasted_iota(jnp.int32, (8, 128), 1)
    load_s.wait()

    @pl.loop(0, ROWS_Z * TILES)
    def _(i):
        z, row = i // TILES, pl.multiple_of((i % TILES) * 8, 8)
        both = [jnp.zeros((8, 128), jnp.float32) for _ in range(2)]
        for f in range(FIELDS):
            half, slot = divmod(f, 16)
            tile = pltpu.roll(pad[f, z + 3, pl.ds(row + 8, 8), :], 3 + 8 * slot, 1)
            both[half] = jnp.where(lane >= 8 * slot, tile, both[half])
        for half in range(2):
            packed[half, z, pl.ds(row, 8), :] = both[half]

    to_left = remote(packed, from_right, y_send.at[0], y_recv.at[0], left)
    to_right = remote(packed, from_left, y_send.at[1], y_recv.at[1], right)

    @pl.when(core == 1)
    def _():
        pl.semaphore_wait(hello.at[1], 2)

    @pl.when(gy > 0)
    def _():
        to_left.start()

    @pl.when(gy < 7)
    def _():
        to_right.start()

    @pl.when(z < 7)
    def _():
        pl.semaphore_wait(hello.at[0], 1)
        to_up.start()

    def start_rest():
        @pl.loop(EARLY, FIELDS)
        def _(n):
            for copy in z_copies(n):
                copy.start()

    @pl.when((gx != 7) & (gx != 8))
    def _():
        start_rest()

    @pl.when((core == 1) & (gx == 0))
    def _():
        pl.semaphore_wait(hello.at[2], 1)

    @pl.when(gx == 0)
    def _():
        for copy in to_mirror:
            copy.start()

    @pl.when(is_first)
    def _():
        pl.semaphore_wait(hello.at[3], 15 - NEAR)
        for q in range(8):
            leg_out(1, q).start()
        pl.semaphore_wait(hello.at[5], 1)
        for q in range(NEAR, 8):
            tell(hello.at[4], in_row(1, q))
        start_rest()

    @pl.when((low == 1) & (z >= NEAR))
    def _():
        pl.semaphore_wait(hello.at[4], 1)
        tell(hello.at[5], last)

    @pl.when(is_last)
    def _():
        pl.semaphore_wait(hello.at[5], 8 - NEAR)
        for q in range(NEAR, 8):
            leg_out(0, q).start()
        start_rest()

    @pl.when(gx < 6)
    def _():
        pl.semaphore_wait(hello.at[4], 1)

    @pl.when((gx > NEAR) & (gx < 7))
    def _():
        tell(hello.at[4], down)

    @pl.when(gx < 7)
    def _():
        leg_out(1, 0).wait_recv()
        leg_in(1).start()

    @pl.when(gx > 8)
    def _():
        leg_out(0, 1).wait_recv()
        leg_in(0).start()

    place = lax.broadcasted_iota(jnp.int32, (ROWS_X, 128), 1) % 8

    @pl.when(gy > 0)
    def _():
        to_right.wait_recv()

    @pl.when(gy < 7)
    def _():
        to_left.wait_recv()

    @pl.when(gy == 0)
    def _():
        @pl.loop(0, 2 * ROWS_Z)
        def _(i):
            own = packed[i // ROWS_Z, i % ROWS_Z]
            from_left[i // ROWS_Z, i % ROWS_Z] = jnp.where(
                place == 0, pltpu.roll(own, 125, 1),
                jnp.where(place == 1, pltpu.roll(own, 126, 1), pltpu.roll(own, 127, 1)),
            )

    @pl.when(gy == 7)
    def _():
        @pl.loop(0, 2 * ROWS_Z)
        def _(i):
            own = packed[i // ROWS_Z, i % ROWS_Z]
            from_right[i // ROWS_Z, i % ROWS_Z] = jnp.where(
                place == 3, pltpu.roll(own, 1, 1),
                jnp.where(place == 4, pltpu.roll(own, 2, 1), pltpu.roll(own, 3, 1)),
            )

    load_b.wait()
    load_f.wait()
    for n in range(len(FIRST)):
        for copy in z_copies(n):
            copy.wait_recv()

    sigma = 0.05 + 0.75 * flag_at[0, 0].astype(jnp.float32)
    damp = sigma * (STEP / 64.0)

    def tile(z, row):
        here = (z + 3, pl.ds(row + 8, 8), slice(None))
        ghosts = [
            jnp.where(lane % 8 < 3, from_left[half, z, pl.ds(row, 8), :], from_right[half, z, pl.ds(row, 8), :])
            for half in range(2)
        ]
        s = [pad[(f,) + here] for f in range(FIELDS)]
        d, dd = {}, {}
        bx, by = s[19] * (STEP / 12.0), s[20] * (STEP / 12.0)
        partial = {}
        for f in FIRST + tuple(f for f in range(FIELDS) if f not in FIRST):
            c = s[f]
            half, slot = divmod(f, 16)
            ghost = pltpu.roll(ghosts[half], (128 - 8 * slot - 3) % 128, 1)
            up = [pad[f, z + 3, pl.ds(row + 8 + k, 8), :] for k in (1, 2, 3)]
            down = [pad[f, z + 3, pl.ds(row + 8 - k, 8), :] for k in (1, 2, 3)]
            right_ = [pltpu.roll(jnp.where(lane < k, ghost, c), 128 - k, 1) for k in (1, 2, 3)]
            left_ = [pltpu.roll(jnp.where(lane >= 128 - k, ghost, c), k, 1) for k in (1, 2, 3)]
            dx = 8.0 * (up[0] - down[0]) - (up[1] - down[1])
            dy = 8.0 * (right_[0] - left_[0]) - (right_[1] - left_[1])
            sx = [up[k] + down[k] for k in range(3)]
            sy = [right_[k] + left_[k] for k in range(3)]
            smooth = (sx[2] + sy[2]) - 6.0 * (sx[1] + sy[1]) + 15.0 * (sx[0] + sy[0]) - 40.0 * c
            partial[f] = bx * dx + by * dy + damp * smooth
            if f in FIRST:
                zs = {k: pad[f, z + 3 + k, pl.ds(row + 8, 8), :] for k in (-2, -1, 1, 2)}
                dz = 8.0 * (zs[1] - zs[-1]) - (zs[2] - zs[-2])
                sz = [zs[1] + zs[-1], zs[2] + zs[-2]]
                d[f] = [v * (1.0 / 12.0) for v in (dx, dy, dz)]
                dd[f] = [(16.0 * v[0] - v[1] - 30.0 * c) * (1.0 / 12.0) for v in (sx, sy, sz)]
        rhs = evolve(s, d, dd)
        for f in range(FIELDS):
            at = (f, z, pl.ds(row, 8), slice(None))
            acc[at] = acc[at] + (partial[f] + STEP * rhs[f])

    @pl.loop(0, 2 * ROWS_Z)
    def _(i):
        tile(i // 2, pl.multiple_of(8 + 8 * (i % 2), 8))

    @pl.when(z > 0)
    def _():
        to_up.wait_recv()

    @pl.when(z < 7)
    def _():
        to_down.wait_recv()

    @pl.when(is_first)
    def _():
        for q in range(8):
            piece(0, q).wait_recv()

    @pl.when(is_last)
    def _():
        for q in range(8):
            piece(1, q).wait_recv()

    @pl.when(gx == 0)
    def _():
        for copy in to_mirror:
            copy.wait_recv()
        turn = jnp.where(
            lax.broadcasted_iota(jnp.int32, (128, 128), 0) + lax.broadcasted_iota(jnp.int32, (128, 128), 1) == 127,
            1.0, 0.0,
        )

        @pl.loop(0, FIELDS)
        def _(f):
            sign = (1 - 2 * ((NEGATIVE_BITS >> f) & 1)).astype(jnp.float32)
            rows = pad[f, 3:11, 0:8, :].reshape(64, 128)
            rows = jnp.dot(rows, turn, precision=lax.Precision.HIGHEST, preferred_element_type=jnp.float32)
            pad[f, 3:11, 0:8, :] = (rows * sign).reshape(8, 8, 128)

    @pl.when(gx == 15)
    def _():
        @pl.loop(0, FIELDS)
        def _(f):
            edge = pad[f, 3:11, 39:40, :]
            pad[f, 3:11, 40:43, :] = jnp.broadcast_to(edge, (8, 3, 128))

    @pl.loop(0, 2 * ROWS_Z)
    def _(i):
        tile(i // 2, pl.multiple_of(24 * (i % 2), 8))

    def along_z(f):
        @pl.loop(0, TILES)
        def _(t):
            row = pl.multiple_of(t * 8, 8)
            v = [pad[f, z, pl.ds(row + 8, 8), :] for z in range(14)]
            for z in range(8):
                w = v[z:z + 7]
                bz = pad[21, z + 3, pl.ds(row + 8, 8), :] * (STEP / 12.0)
                dz = 8.0 * (w[4] - w[2]) - (w[5] - w[1])
                smooth = (w[6] + w[0]) - 6.0 * (w[5] + w[1]) + 15.0 * (w[4] + w[2]) - 20.0 * w[3]
                at = (f, z, pl.ds(row, 8), slice(None))
                acc[at] = acc[at] + (bz * dz + damp * smooth)

    @pl.loop(0, FIELDS)
    def _(n):
        @pl.when(n >= len(FIRST))
        def _():
            for copy in z_copies(n):
                copy.wait_recv()

        along_z(field_at(n))
        for copy in z_copies(n):
            copy.wait_send()

    @pl.when(z > 0)
    def _():
        to_down.wait_send()

    @pl.when(z < 7)
    def _():
        to_up.wait_send()

    @pl.when(gx == 0)
    def _():
        for copy in to_mirror:
            copy.wait_send()

    @pl.when(is_last)
    def _():
        for q in range(8):
            leg_out(0, q).wait_send()

    @pl.when(is_first)
    def _():
        for q in range(8):
            leg_out(1, q).wait_send()

    @pl.when((gx != 7) & (gx != 8))
    def _():
        piece(0, 0).wait_send()

    @pl.when(gy > 0)
    def _():
        to_left.wait_send()

    @pl.when(gy < 7)
    def _():
        to_right.wait_send()


def body(section_fields, base_fields, flags):
    f32 = jnp.float32
    block = (FIELDS, ROWS_Z, ROWS_X, ROWS_Y)
    dma = pltpu.SemaphoreType.DMA
    return pl.pallas_call(
        kernel,
        out_shape=jax.ShapeDtypeStruct(block, f32),
        in_specs=[
            pl.BlockSpec(memory_space=pl.ANY),
            pl.BlockSpec(memory_space=pl.ANY),
            pl.BlockSpec(memory_space=pl.ANY),
        ],
        out_specs=pl.BlockSpec(memory_space=pltpu.VMEM),
        scratch_shapes=[
            pltpu.VMEM((FIELDS, 14, 48, ROWS_Y), f32),
            pltpu.VMEM((FIELDS, 8, ROWS_Y), f32),
            pltpu.VMEM((2, ROWS_Z, ROWS_X, ROWS_Y), f32),
            pltpu.VMEM((2, ROWS_Z, ROWS_X, ROWS_Y), f32),
            pltpu.VMEM((2, ROWS_Z, ROWS_X, ROWS_Y), f32),
            pltpu.SMEM((1, 1), jnp.int32),
            dma((3,)),
            dma((2, FIELDS)),
            dma((2, FIELDS)),
            dma((5,)),
            dma((5,)),
            dma((2,)),
            dma((2,)),
            dma((9,)),
            dma((1,)),
            dma((8,)),
            pltpu.SemaphoreType.REGULAR((6,)),
        ],
        compiler_params=pltpu.CompilerParams(
            collective_id=0, has_side_effects=True, vmem_limit_bytes=48 * 2**20
        ),
        cost_estimate=pl.CostEstimate(flops=80_000_000, bytes_accessed=9_830_400, transcendentals=0),
        name="substep",
    )(section_fields, base_fields, flags)


def solution(mesh):
    spec = P(None, "gz", "gx", "gy")
    return jax.shard_map(
        body, mesh=mesh, in_specs=(spec, spec, P("gx", "gy")), out_specs=spec, check_vma=False
    )
```

```python
import jax
import jax.numpy as jnp
from jax import lax
from jax.experimental import pallas as pl
from jax.experimental.pallas import tpu as pltpu
from jax.sharding import PartitionSpec as P

MESH = pl.DeviceIdType.MESH
FIELDS = 25
PAIRS = ((0, 0), (0, 1), (0, 2), (1, 1), (1, 2), (2, 2))
NEGATIVE = (3, 5, 10, 12, 14, 15, 19, 20, 22, 23)
NEGATIVE_BITS = sum(1 << c for c in NEGATIVE)
FIRST = (17, 19, 20, 21)
EARLY = 8
NEAR = 2
ROWS_Z, ROWS_X, ROWS_Y = 8, 32, 128
TILES = ROWS_X // 8
STEP = 0.25


def field_at(n):
    rest = jnp.where(n < 21, n - 4, jnp.where(n < 22, 18, n))
    return jnp.where(n < 1, 17, jnp.where(n < 4, 18 + n, rest))


def remote(src, dst, send, recv, device):
    return pltpu.make_async_remote_copy(
        src_ref=src, dst_ref=dst, send_sem=send, recv_sem=recv, device_id=device, device_id_type=MESH
    )


def sym(i, j):
    return PAIRS.index((min(i, j), max(i, j)))


def evolve(s, d, dd):
    chi, trace, lapse, theta = s[0], s[7], s[17], s[18]
    g = lambda i, j: s[1 + sym(i, j)]
    a = lambda i, j: s[8 + sym(i, j)]
    grad = lambda k, j: d[19 + k][j]
    div = grad(0, 0) + grad(1, 1) + grad(2, 2)
    lap = dd[17][0] + dd[17][1] + dd[17][2]
    div23 = (2.0 / 3.0) * div
    square = (
        a(0, 0) * a(0, 0) + a(1, 1) * a(1, 1) + a(2, 2) * a(2, 2)
        + 2.0 * (a(0, 1) * a(0, 1) + a(0, 2) * a(0, 2) + a(1, 2) * a(1, 2))
    )
    out = {}
    out[0] = chi * ((2.0 / 3.0) * (lapse * trace) - div23)
    lapse2 = 2.0 * lapse
    for n, (i, j) in enumerate(PAIRS):
        if i == j:
            lie_g = 2.0 * sum(g(i, k) * grad(k, i) for k in range(3))
            lie_a = 2.0 * sum(a(i, k) * grad(k, i) for k in range(3))
        else:
            lie_g = sum(g(i, k) * grad(k, j) + g(j, k) * grad(k, i) for k in range(3))
            lie_a = sum(a(i, k) * grad(k, j) + a(j, k) * grad(k, i) for k in range(3))
        out[1 + n] = lie_g - lapse2 * a(i, j) - g(i, j) * div23
        quad = sum(a(i, k) * a(k, j) for k in range(3))
        term = lapse * (trace * a(i, j)) - lapse2 * quad + lie_a - a(i, j) * div23
        if i == j:
            term = term + chi * (lap * (1.0 / 3.0) - dd[17][i])
        out[8 + n] = term
    third = trace * trace * (1.0 / 3.0)
    out[7] = lapse * (square + third) - chi * lap
    for i in range(3):
        value = dd[19 + i][0] + dd[19 + i][1] + dd[19 + i][2]
        value = value - 2.0 * sum(a(i, j) * d[17][j] for j in range(3))
        value = value + s[14 + i] * div23
        value = value - sum(s[14 + j] * grad(i, j) for j in range(3))
        out[14 + i] = value
        out[22 + i] = value - 2.0 * s[22 + i]
        out[19 + i] = 0.75 * s[22 + i]
    out[17] = -lapse2 * (trace - 2.0 * theta)
    out[18] = lapse * (third - 0.5 * square) - 0.04 * (lapse * theta)
    return out


def kernel(
    sec, base, flag, acc,
    pad, cross, packed, from_left, from_right, flag_at,
    load_sem, z_send, z_recv, x_send, x_recv, y_send, y_recv, leg_send, leg_recv, arrive_recv, hello,
):
    gx, gy, gz = lax.axis_index("gx"), lax.axis_index("gy"), lax.axis_index("gz")
    low, z, core = gx // 8, gx % 8, gy % 2
    partner = (gx, gy, 1 - gz)
    left, right = (gx, (gy + 7) % 8, gz), (gx, (gy + 1) % 8, gz)
    up, down = (gx + 1, gy, gz), (gx - 1, gy, gz)
    mirror = (0, 7 - gy, gz)
    last, first = (7, gy, gz), (8, gy, gz)
    is_last, is_first = gx == 7, gx == 8
    in_row = lambda half, q: (8 * half + q, gy, gz)

    load_s = pltpu.make_async_copy(sec, pad.at[:, 3:11, 8:40, :], load_sem.at[0])
    load_b = pltpu.make_async_copy(base, acc, load_sem.at[1])
    load_f = pltpu.make_async_copy(flag, flag_at, load_sem.at[2])
    barrier = pltpu.get_barrier_semaphore()

    def tell(semaphore, device):
        pl.semaphore_signal(semaphore, inc=1, device_id=device, device_id_type=MESH)

    tell(barrier, partner)
    load_f.start()

    @pl.when(core == 1)
    def _():
        tell(barrier, left)
        tell(barrier, right)

    @pl.when((core == 1) & (gx == 0))
    def _():
        tell(barrier, mirror)

    @pl.when(z < 4)
    def _():
        tell(barrier, up)

    @pl.when(z == 0)
    def _():
        for q in range(4, 8):
            tell(barrier, (gx + q, gy, gz))

    @pl.when(z < NEAR)
    def _():
        tell(barrier, last)

    @pl.when(gx == 0)
    def _():
        tell(barrier, first)

    @pl.when(is_first)
    def _():
        for q in range(8):
            if q > 0:
                tell(barrier, in_row(0, q))
                tell(barrier, in_row(1, q))

    expected = (
        1 + jnp.where(core == 0, 2, 0) + jnp.where((core == 0) & (gx == 0), 1, 0) + jnp.where(z > 0, 1, 0) + jnp.where(z == 4, 1, 0)
        + jnp.where(is_last, 2 * NEAR, 0) + jnp.where(gx == 0, 0, 1)
    )
    pl.semaphore_wait(barrier, expected)

    def z_copies(n):
        f = field_at(n)
        return (
            remote(sec.at[f, 0:3], pad.at[f, 11:14, 8:40, :], z_send.at[0, n], z_recv.at[0, n], partner),
            remote(sec.at[f, 5:8], pad.at[f, 0:3, 8:40, :], z_send.at[1, n], z_recv.at[1, n], partner),
        )

    @pl.loop(0, EARLY)
    def _(n):
        for copy in z_copies(n):
            copy.start()

    def start_rest():
        @pl.loop(EARLY, FIELDS)
        def _(n):
            for copy in z_copies(n):
                copy.start()

    @pl.when((gx != 7) & (gx != 8))
    def _():
        start_rest()

    load_s.start()

    @pl.when((z > 0) & (z < 5))
    def _():
        tell(hello.at[0], down)

    @pl.when(z > 3)
    def _():
        tell(hello.at[0], (gx - z, gy, gz))

    @pl.when(core == 0)
    def _():
        tell(hello.at[1], left)
        tell(hello.at[1], right)

    @pl.when((core == 0) & (gx == 0))
    def _():
        tell(hello.at[2], mirror)

    @pl.when(((low == 0) & (z > 0)) | (z >= NEAR))
    def _():
        tell(hello.at[3], first)

    @pl.when(is_last)
    def _():
        for q in range(NEAR):
            tell(hello.at[4], in_row(0, q))
        tell(hello.at[5], first)

    to_up = remote(sec.at[:, :, 29:32, :], pad.at[:, 3:11, 5:8, :], x_send.at[3], x_recv.at[3], up)
    to_down = remote(sec.at[:, :, 0:3, :], pad.at[:, 3:11, 40:43, :], x_send.at[4], x_recv.at[4], down)
    to_mirror = [
        remote(sec.at[:, :, i:i + 1, :], pad.at[:, 3:11, 7 - i:8 - i, :], x_send.at[i], x_recv.at[i], mirror)
        for i in range(3)
    ]

    def leg_out(half, q):
        rows = slice(29, 32) if half == 0 else slice(0, 3)
        own = q == 7 * half
        ghost = piece_ghost(half, q) if own else cross.at[:, 0:3, :]
        return remote(
            sec.at[:, q, rows, :], ghost, leg_send.at[q], arrive_recv.at[q] if own else leg_recv.at[0], in_row(1 - half, q)
        )

    def piece_ghost(half, q):
        return pad.at[:, 3 + q, 5:8, :] if half == 0 else pad.at[:, 3 + q, 40:43, :]

    def leg_in(half):
        return remote(
            cross.at[:, 0:3, :], piece_ghost(half, z), leg_send.at[8], arrive_recv.at[z], first if half == 0 else last
        )

    def piece(half, q):
        return remote(cross.at[:, 0:3, :], piece_ghost(half, q), leg_send.at[8], arrive_recv.at[q], first)

    @pl.when((z > 0) & (z < 5))
    def _():
        to_down.start()

    @pl.when(is_last)
    def _():
        for q in range(NEAR):
            leg_out(0, q).start()

    lane = lax.broadcasted_iota(jnp.int32, (8, 128), 1)
    load_s.wait()

    @pl.loop(0, ROWS_Z * TILES)
    def _(i):
        z, row = i // TILES, pl.multiple_of((i % TILES) * 8, 8)
        both = [jnp.zeros((8, 128), jnp.float32) for _ in range(2)]
        for f in range(FIELDS):
            half, slot = divmod(f, 16)
            tile = pltpu.roll(pad[f, z + 3, pl.ds(row + 8, 8), :], 3 + 8 * slot, 1)
            both[half] = jnp.where(lane >= 8 * slot, tile, both[half])
        for half in range(2):
            packed[half, z, pl.ds(row, 8), :] = both[half]

    to_left = remote(packed, from_right, y_send.at[0], y_recv.at[0], left)
    to_right = remote(packed, from_left, y_send.at[1], y_recv.at[1], right)

    @pl.when(core == 1)
    def _():
        pl.semaphore_wait(hello.at[1], 2)

    @pl.when(gy > 0)
    def _():
        to_left.start()

    @pl.when(gy < 7)
    def _():
        to_right.start()

    @pl.when(z == 0)
    def _():
        pl.semaphore_wait(hello.at[0], 5)
        for q in range(4, 8):
            tell(hello.at[0], (gx + q, gy, gz))

    @pl.when(z > 0)
    def _():
        pl.semaphore_wait(hello.at[0], 1)

    @pl.when(z < 7)
    def _():
        to_up.start()

    @pl.when(z > 4)
    def _():
        to_down.start()

    @pl.when((core == 1) & (gx == 0))
    def _():
        pl.semaphore_wait(hello.at[2], 1)

    @pl.when(gx == 0)
    def _():
        for copy in to_mirror:
            copy.start()

    @pl.when(is_first)
    def _():
        pl.semaphore_wait(hello.at[3], 15 - NEAR)
        for q in range(8):
            leg_out(1, q).start()
        pl.semaphore_wait(hello.at[5], 1)
        for q in range(NEAR, 8):
            tell(hello.at[4], in_row(1, q))
        start_rest()

    @pl.when((low == 1) & (z >= NEAR))
    def _():
        pl.semaphore_wait(hello.at[4], 1)
        tell(hello.at[5], last)

    @pl.when(is_last)
    def _():
        pl.semaphore_wait(hello.at[5], 8 - NEAR)
        for q in range(NEAR, 8):
            leg_out(0, q).start()
        start_rest()

    @pl.when(gx < 6)
    def _():
        pl.semaphore_wait(hello.at[4], 1)

    @pl.when((gx > NEAR) & (gx < 7))
    def _():
        tell(hello.at[4], down)

    @pl.when(gx < 7)
    def _():
        leg_out(1, 0).wait_recv()
        leg_in(1).start()

    @pl.when(gx > 8)
    def _():
        leg_out(0, 1).wait_recv()
        leg_in(0).start()

    load_b.start()

    place = lax.broadcasted_iota(jnp.int32, (ROWS_X, 128), 1) % 8

    @pl.when(gy > 0)
    def _():
        to_right.wait_recv()

    @pl.when(gy < 7)
    def _():
        to_left.wait_recv()

    @pl.when(gy == 0)
    def _():
        @pl.loop(0, 2 * ROWS_Z)
        def _(i):
            own = packed[i // ROWS_Z, i % ROWS_Z]
            from_left[i // ROWS_Z, i % ROWS_Z] = jnp.where(
                place == 0, pltpu.roll(own, 125, 1),
                jnp.where(place == 1, pltpu.roll(own, 126, 1), pltpu.roll(own, 127, 1)),
            )

    @pl.when(gy == 7)
    def _():
        @pl.loop(0, 2 * ROWS_Z)
        def _(i):
            own = packed[i // ROWS_Z, i % ROWS_Z]
            from_right[i // ROWS_Z, i % ROWS_Z] = jnp.where(
                place == 3, pltpu.roll(own, 1, 1),
                jnp.where(place == 4, pltpu.roll(own, 2, 1), pltpu.roll(own, 3, 1)),
            )

    load_b.wait()
    load_f.wait()
    for n in range(len(FIRST)):
        for copy in z_copies(n):
            copy.wait_recv()

    sigma = 0.05 + 0.75 * flag_at[0, 0].astype(jnp.float32)
    damp = sigma * (STEP / 64.0)

    def tile(z, row):
        here = (z + 3, pl.ds(row + 8, 8), slice(None))
        ghosts = [
            jnp.where(lane % 8 < 3, from_left[half, z, pl.ds(row, 8), :], from_right[half, z, pl.ds(row, 8), :])
            for half in range(2)
        ]
        s = [pad[(f,) + here] for f in range(FIELDS)]
        d, dd = {}, {}
        bx, by = s[19] * (STEP / 12.0), s[20] * (STEP / 12.0)
        partial = {}
        for f in FIRST + tuple(f for f in range(FIELDS) if f not in FIRST):
            c = s[f]
            half, slot = divmod(f, 16)
            ghost = pltpu.roll(ghosts[half], (128 - 8 * slot - 3) % 128, 1)
            up = [pad[f, z + 3, pl.ds(row + 8 + k, 8), :] for k in (1, 2, 3)]
            down = [pad[f, z + 3, pl.ds(row + 8 - k, 8), :] for k in (1, 2, 3)]
            right_ = [pltpu.roll(jnp.where(lane < k, ghost, c), 128 - k, 1) for k in (1, 2, 3)]
            left_ = [pltpu.roll(jnp.where(lane >= 128 - k, ghost, c), k, 1) for k in (1, 2, 3)]
            dx = 8.0 * (up[0] - down[0]) - (up[1] - down[1])
            dy = 8.0 * (right_[0] - left_[0]) - (right_[1] - left_[1])
            sx = [up[k] + down[k] for k in range(3)]
            sy = [right_[k] + left_[k] for k in range(3)]
            smooth = (sx[2] + sy[2]) - 6.0 * (sx[1] + sy[1]) + 15.0 * (sx[0] + sy[0]) - 40.0 * c
            partial[f] = bx * dx + by * dy + damp * smooth
            if f in FIRST:
                zs = {k: pad[f, z + 3 + k, pl.ds(row + 8, 8), :] for k in (-2, -1, 1, 2)}
                dz = 8.0 * (zs[1] - zs[-1]) - (zs[2] - zs[-2])
                sz = [zs[1] + zs[-1], zs[2] + zs[-2]]
                d[f] = [v * (1.0 / 12.0) for v in (dx, dy, dz)]
                dd[f] = [(16.0 * v[0] - v[1] - 30.0 * c) * (1.0 / 12.0) for v in (sx, sy, sz)]
        rhs = evolve(s, d, dd)
        for f in range(FIELDS):
            at = (f, z, pl.ds(row, 8), slice(None))
            acc[at] = acc[at] + (partial[f] + STEP * rhs[f])

    @pl.loop(0, 2 * ROWS_Z)
    def _(i):
        tile(i // 2, pl.multiple_of(8 + 8 * (i % 2), 8))

    @pl.when(z > 0)
    def _():
        to_up.wait_recv()

    @pl.when(z < 7)
    def _():
        to_down.wait_recv()

    @pl.when(is_first)
    def _():
        for q in range(8):
            piece(0, q).wait_recv()

    @pl.when(is_last)
    def _():
        for q in range(8):
            piece(1, q).wait_recv()

    @pl.when(gx == 0)
    def _():
        for copy in to_mirror:
            copy.wait_recv()
        turn = jnp.where(
            lax.broadcasted_iota(jnp.int32, (128, 128), 0) + lax.broadcasted_iota(jnp.int32, (128, 128), 1) == 127,
            1.0, 0.0,
        )

        @pl.loop(0, FIELDS)
        def _(f):
            sign = (1 - 2 * ((NEGATIVE_BITS >> f) & 1)).astype(jnp.float32)
            rows = pad[f, 3:11, 0:8, :].reshape(64, 128)
            rows = jnp.dot(rows, turn, precision=lax.Precision.HIGHEST, preferred_element_type=jnp.float32)
            pad[f, 3:11, 0:8, :] = (rows * sign).reshape(8, 8, 128)

    @pl.when(gx == 15)
    def _():
        @pl.loop(0, FIELDS)
        def _(f):
            edge = pad[f, 3:11, 39:40, :]
            pad[f, 3:11, 40:43, :] = jnp.broadcast_to(edge, (8, 3, 128))

    @pl.loop(0, 2 * ROWS_Z)
    def _(i):
        tile(i // 2, pl.multiple_of(24 * (i % 2), 8))

    @pl.when(z > 0)
    def _():
        to_down.wait_send()

    @pl.when(z < 7)
    def _():
        to_up.wait_send()

    @pl.when(gx == 0)
    def _():
        for copy in to_mirror:
            copy.wait_send()

    @pl.when(is_last)
    def _():
        for q in range(8):
            leg_out(0, q).wait_send()

    @pl.when(is_first)
    def _():
        for q in range(8):
            leg_out(1, q).wait_send()

    @pl.when((gx != 7) & (gx != 8))
    def _():
        piece(0, 0).wait_send()

    @pl.when(gy > 0)
    def _():
        to_left.wait_send()

    @pl.when(gy < 7)
    def _():
        to_right.wait_send()

    def along_z(f):
        @pl.loop(0, TILES)
        def _(t):
            row = pl.multiple_of(t * 8, 8)
            v = [pad[f, z, pl.ds(row + 8, 8), :] for z in range(14)]
            for z in range(8):
                w = v[z:z + 7]
                bz = pad[21, z + 3, pl.ds(row + 8, 8), :] * (STEP / 12.0)
                dz = 8.0 * (w[4] - w[2]) - (w[5] - w[1])
                smooth = (w[6] + w[0]) - 6.0 * (w[5] + w[1]) + 15.0 * (w[4] + w[2]) - 20.0 * w[3]
                at = (f, z, pl.ds(row, 8), slice(None))
                acc[at] = acc[at] + (bz * dz + damp * smooth)

    @pl.loop(0, FIELDS)
    def _(n):
        @pl.when(n >= len(FIRST))
        def _():
            for copy in z_copies(n):
                copy.wait_recv()

        along_z(field_at(n))
        for copy in z_copies(n):
            copy.wait_send()


def body(section_fields, base_fields, flags):
    f32 = jnp.float32
    block = (FIELDS, ROWS_Z, ROWS_X, ROWS_Y)
    dma = pltpu.SemaphoreType.DMA
    return pl.pallas_call(
        kernel,
        out_shape=jax.ShapeDtypeStruct(block, f32),
        in_specs=[
            pl.BlockSpec(memory_space=pl.ANY),
            pl.BlockSpec(memory_space=pl.ANY),
            pl.BlockSpec(memory_space=pl.ANY),
        ],
        out_specs=pl.BlockSpec(memory_space=pltpu.VMEM),
        scratch_shapes=[
            pltpu.VMEM((FIELDS, 14, 48, ROWS_Y), f32),
            pltpu.VMEM((FIELDS, 8, ROWS_Y), f32),
            pltpu.VMEM((2, ROWS_Z, ROWS_X, ROWS_Y), f32),
            pltpu.VMEM((2, ROWS_Z, ROWS_X, ROWS_Y), f32),
            pltpu.VMEM((2, ROWS_Z, ROWS_X, ROWS_Y), f32),
            pltpu.SMEM((1, 1), jnp.int32),
            dma((3,)),
            dma((2, FIELDS)),
            dma((2, FIELDS)),
            dma((5,)),
            dma((5,)),
            dma((2,)),
            dma((2,)),
            dma((9,)),
            dma((1,)),
            dma((8,)),
            pltpu.SemaphoreType.REGULAR((6,)),
        ],
        compiler_params=pltpu.CompilerParams(
            collective_id=0, has_side_effects=True, vmem_limit_bytes=48 * 2**20
        ),
        cost_estimate=pl.CostEstimate(flops=80_000_000, bytes_accessed=9_830_400, transcendentals=0),
        name="substep",
    )(section_fields, base_fields, flags)


def solution(mesh):
    spec = P(None, "gz", "gx", "gy")
    return jax.shard_map(
        body, mesh=mesh, in_specs=(spec, spec, P("gx", "gy")), out_specs=spec, check_vma=False
    )
```

```python
import jax
import jax.numpy as jnp
from jax import lax
from jax.experimental import pallas as pl
from jax.experimental.pallas import tpu as pltpu
from jax.sharding import PartitionSpec as P

MESH = pl.DeviceIdType.MESH
FIELDS = 25
PAIRS = ((0, 0), (0, 1), (0, 2), (1, 1), (1, 2), (2, 2))
NEGATIVE = (3, 5, 10, 12, 14, 15, 19, 20, 22, 23)
NEGATIVE_BITS = sum(1 << c for c in NEGATIVE)
FIRST = (17, 19, 20, 21)
EARLY = 8
NEAR = 2
ROWS_Z, ROWS_X, ROWS_Y = 8, 32, 128
TILES = ROWS_X // 8
STEP = 0.25


def field_at(n):
    rest = jnp.where(n < 21, n - 4, jnp.where(n < 22, 18, n))
    return jnp.where(n < 1, 17, jnp.where(n < 4, 18 + n, rest))


def remote(src, dst, send, recv, device):
    return pltpu.make_async_remote_copy(
        src_ref=src, dst_ref=dst, send_sem=send, recv_sem=recv, device_id=device, device_id_type=MESH
    )


def sym(i, j):
    return PAIRS.index((min(i, j), max(i, j)))


def evolve(s, d, dd):
    chi, trace, lapse, theta = s[0], s[7], s[17], s[18]
    g = lambda i, j: s[1 + sym(i, j)]
    a = lambda i, j: s[8 + sym(i, j)]
    grad = lambda k, j: d[19 + k][j]
    div = grad(0, 0) + grad(1, 1) + grad(2, 2)
    lap = dd[17][0] + dd[17][1] + dd[17][2]
    div23 = (2.0 / 3.0) * div
    square = (
        a(0, 0) * a(0, 0) + a(1, 1) * a(1, 1) + a(2, 2) * a(2, 2)
        + 2.0 * (a(0, 1) * a(0, 1) + a(0, 2) * a(0, 2) + a(1, 2) * a(1, 2))
    )
    out = {}
    out[0] = chi * ((2.0 / 3.0) * (lapse * trace) - div23)
    lapse2 = 2.0 * lapse
    for n, (i, j) in enumerate(PAIRS):
        if i == j:
            lie_g = 2.0 * sum(g(i, k) * grad(k, i) for k in range(3))
            lie_a = 2.0 * sum(a(i, k) * grad(k, i) for k in range(3))
        else:
            lie_g = sum(g(i, k) * grad(k, j) + g(j, k) * grad(k, i) for k in range(3))
            lie_a = sum(a(i, k) * grad(k, j) + a(j, k) * grad(k, i) for k in range(3))
        out[1 + n] = lie_g - lapse2 * a(i, j) - g(i, j) * div23
        quad = sum(a(i, k) * a(k, j) for k in range(3))
        term = lapse * (trace * a(i, j)) - lapse2 * quad + lie_a - a(i, j) * div23
        if i == j:
            term = term + chi * (lap * (1.0 / 3.0) - dd[17][i])
        out[8 + n] = term
    third = trace * trace * (1.0 / 3.0)
    out[7] = lapse * (square + third) - chi * lap
    for i in range(3):
        value = dd[19 + i][0] + dd[19 + i][1] + dd[19 + i][2]
        value = value - 2.0 * sum(a(i, j) * d[17][j] for j in range(3))
        value = value + s[14 + i] * div23
        value = value - sum(s[14 + j] * grad(i, j) for j in range(3))
        out[14 + i] = value
        out[22 + i] = value - 2.0 * s[22 + i]
        out[19 + i] = 0.75 * s[22 + i]
    out[17] = -lapse2 * (trace - 2.0 * theta)
    out[18] = lapse * (third - 0.5 * square) - 0.04 * (lapse * theta)
    return out


def kernel(
    sec, base, flag, acc,
    pad, cross, packed, from_left, from_right, flag_at,
    load_sem, z_send, z_recv, x_send, x_recv, y_send, y_recv, leg_send, leg_recv, arrive_recv, hello,
):
    gx, gy, gz = lax.axis_index("gx"), lax.axis_index("gy"), lax.axis_index("gz")
    low, z, core = gx // 8, gx % 8, gy % 2
    partner = (gx, gy, 1 - gz)
    left, right = (gx, (gy + 7) % 8, gz), (gx, (gy + 1) % 8, gz)
    up, down = (gx + 1, gy, gz), (gx - 1, gy, gz)
    mirror = (0, 7 - gy, gz)
    last, first = (7, gy, gz), (8, gy, gz)
    is_last, is_first = gx == 7, gx == 8
    in_row = lambda half, q: (8 * half + q, gy, gz)

    load_s = pltpu.make_async_copy(sec, pad.at[:, 3:11, 8:40, :], load_sem.at[0])
    load_b = pltpu.make_async_copy(base, acc, load_sem.at[1])
    load_f = pltpu.make_async_copy(flag, flag_at, load_sem.at[2])
    barrier = pltpu.get_barrier_semaphore()

    def tell(semaphore, device):
        pl.semaphore_signal(semaphore, inc=1, device_id=device, device_id_type=MESH)

    tell(barrier, partner)
    load_f.start()

    @pl.when(core == 1)
    def _():
        tell(barrier, left)
        tell(barrier, right)

    @pl.when((core == 1) & (gx == 0))
    def _():
        tell(barrier, mirror)

    @pl.when(z < 4)
    def _():
        tell(barrier, up)

    @pl.when(z == 0)
    def _():
        for q in range(4, 8):
            tell(barrier, (gx + q, gy, gz))

    @pl.when(z < NEAR)
    def _():
        tell(barrier, last)

    @pl.when(gx == 0)
    def _():
        tell(barrier, first)

    @pl.when(is_first)
    def _():
        for q in range(8):
            if q > 0:
                tell(barrier, in_row(0, q))
                tell(barrier, in_row(1, q))

    expected = (
        1 + jnp.where(core == 0, 2, 0) + jnp.where((core == 0) & (gx == 0), 1, 0) + jnp.where(z > 0, 1, 0) + jnp.where(z == 4, 1, 0)
        + jnp.where(is_last, 2 * NEAR, 0) + jnp.where(gx == 0, 0, 1)
    )
    pl.semaphore_wait(barrier, expected)

    def z_copies(n):
        f = field_at(n)
        return (
            remote(sec.at[f, 0:3], pad.at[f, 11:14, 8:40, :], z_send.at[0, n], z_recv.at[0, n], partner),
            remote(sec.at[f, 5:8], pad.at[f, 0:3, 8:40, :], z_send.at[1, n], z_recv.at[1, n], partner),
        )

    @pl.loop(0, EARLY)
    def _(n):
        for copy in z_copies(n):
            copy.start()

    def start_rest():
        @pl.loop(EARLY, FIELDS)
        def _(n):
            for copy in z_copies(n):
                copy.start()

    @pl.when((gx != 7) & (gx != 8))
    def _():
        start_rest()

    load_s.start()

    @pl.when((z > 0) & (z < 5))
    def _():
        tell(hello.at[0], down)

    @pl.when(z > 3)
    def _():
        tell(hello.at[0], (gx - z, gy, gz))

    @pl.when(core == 0)
    def _():
        tell(hello.at[1], left)
        tell(hello.at[1], right)

    @pl.when((core == 0) & (gx == 0))
    def _():
        tell(hello.at[2], mirror)

    @pl.when(((low == 0) & (z > 0)) | (z >= NEAR))
    def _():
        tell(hello.at[3], first)

    @pl.when(is_last)
    def _():
        for q in range(NEAR):
            tell(hello.at[4], in_row(0, q))
        tell(hello.at[5], first)

    to_up = remote(sec.at[:, :, 29:32, :], pad.at[:, 3:11, 5:8, :], x_send.at[3], x_recv.at[3], up)
    to_down = remote(sec.at[:, :, 0:3, :], pad.at[:, 3:11, 40:43, :], x_send.at[4], x_recv.at[4], down)
    to_mirror = [
        remote(sec.at[:, :, i:i + 1, :], pad.at[:, 3:11, 7 - i:8 - i, :], x_send.at[i], x_recv.at[i], mirror)
        for i in range(3)
    ]

    def leg_out(half, q):
        rows = slice(29, 32) if half == 0 else slice(0, 3)
        own = q == 7 * half
        ghost = piece_ghost(half, q) if own else cross.at[:, 0:3, :]
        return remote(
            sec.at[:, q, rows, :], ghost, leg_send.at[q], arrive_recv.at[q] if own else leg_recv.at[0], in_row(1 - half, q)
        )

    def piece_ghost(half, q):
        return pad.at[:, 3 + q, 5:8, :] if half == 0 else pad.at[:, 3 + q, 40:43, :]

    def leg_in(half):
        return remote(
            cross.at[:, 0:3, :], piece_ghost(half, z), leg_send.at[8], arrive_recv.at[z], first if half == 0 else last
        )

    def piece(half, q):
        return remote(cross.at[:, 0:3, :], piece_ghost(half, q), leg_send.at[8], arrive_recv.at[q], first)

    @pl.when((z > 0) & (z < 5))
    def _():
        to_down.start()

    @pl.when(is_last)
    def _():
        for q in range(NEAR):
            leg_out(0, q).start()

    lane = lax.broadcasted_iota(jnp.int32, (8, 128), 1)
    load_s.wait()

    @pl.loop(0, ROWS_Z * TILES)
    def _(i):
        z, row = i // TILES, pl.multiple_of((i % TILES) * 8, 8)
        both = [jnp.zeros((8, 128), jnp.float32) for _ in range(2)]
        for f in range(FIELDS):
            half, slot = divmod(f, 16)
            tile = pltpu.roll(pad[f, z + 3, pl.ds(row + 8, 8), :], 3 + 8 * slot, 1)
            both[half] = jnp.where(lane >= 8 * slot, tile, both[half])
        for half in range(2):
            packed[half, z, pl.ds(row, 8), :] = both[half]

    to_left = remote(packed, from_right, y_send.at[0], y_recv.at[0], left)
    to_right = remote(packed, from_left, y_send.at[1], y_recv.at[1], right)

    @pl.when(core == 1)
    def _():
        pl.semaphore_wait(hello.at[1], 2)

    @pl.when(gy > 0)
    def _():
        to_left.start()

    @pl.when(gy < 7)
    def _():
        to_right.start()

    @pl.when(z == 0)
    def _():
        pl.semaphore_wait(hello.at[0], 5)
        for q in range(4, 8):
            tell(hello.at[0], (gx + q, gy, gz))

    @pl.when(z > 0)
    def _():
        pl.semaphore_wait(hello.at[0], 1)

    @pl.when(z < 7)
    def _():
        to_up.start()

    @pl.when(z > 4)
    def _():
        to_down.start()

    @pl.when((core == 1) & (gx == 0))
    def _():
        pl.semaphore_wait(hello.at[2], 1)

    @pl.when(gx == 0)
    def _():
        for copy in to_mirror:
            copy.start()

    @pl.when(is_first)
    def _():
        pl.semaphore_wait(hello.at[3], 15 - NEAR)
        for q in range(8):
            leg_out(1, q).start()
        pl.semaphore_wait(hello.at[5], 1)
        for q in range(NEAR, 8):
            tell(hello.at[4], in_row(1, q))
        start_rest()

    @pl.when((low == 1) & (z >= NEAR))
    def _():
        pl.semaphore_wait(hello.at[4], 1)
        tell(hello.at[5], last)

    @pl.when(is_last)
    def _():
        pl.semaphore_wait(hello.at[5], 8 - NEAR)
        for q in range(NEAR, 8):
            leg_out(0, q).start()
        start_rest()

    @pl.when(gx < 6)
    def _():
        pl.semaphore_wait(hello.at[4], 1)

    @pl.when((gx > NEAR) & (gx < 7))
    def _():
        tell(hello.at[4], down)

    @pl.when(gx < 7)
    def _():
        leg_out(1, 0).wait_recv()
        leg_in(1).start()

    @pl.when(gx > 8)
    def _():
        leg_out(0, 1).wait_recv()
        leg_in(0).start()

    load_b.start()

    place = lax.broadcasted_iota(jnp.int32, (ROWS_X, 128), 1) % 8

    @pl.when(gy > 0)
    def _():
        to_right.wait_recv()

    @pl.when(gy < 7)
    def _():
        to_left.wait_recv()

    @pl.when(gy == 0)
    def _():
        @pl.loop(0, 2 * ROWS_Z)
        def _(i):
            own = packed[i // ROWS_Z, i % ROWS_Z]
            from_left[i // ROWS_Z, i % ROWS_Z] = jnp.where(
                place == 0, pltpu.roll(own, 125, 1),
                jnp.where(place == 1, pltpu.roll(own, 126, 1), pltpu.roll(own, 127, 1)),
            )

    @pl.when(gy == 7)
    def _():
        @pl.loop(0, 2 * ROWS_Z)
        def _(i):
            own = packed[i // ROWS_Z, i % ROWS_Z]
            from_right[i // ROWS_Z, i % ROWS_Z] = jnp.where(
                place == 3, pltpu.roll(own, 1, 1),
                jnp.where(place == 4, pltpu.roll(own, 2, 1), pltpu.roll(own, 3, 1)),
            )

    load_b.wait()
    load_f.wait()
    for n in range(len(FIRST)):
        for copy in z_copies(n):
            copy.wait_recv()

    sigma = 0.05 + 0.75 * flag_at[0, 0].astype(jnp.float32)
    damp = sigma * (STEP / 64.0)

    def tile(z, row):
        here = (z + 3, pl.ds(row + 8, 8), slice(None))
        ghosts = [
            jnp.where(lane % 8 < 3, from_left[half, z, pl.ds(row, 8), :], from_right[half, z, pl.ds(row, 8), :])
            for half in range(2)
        ]
        s = [pad[(f,) + here] for f in range(FIELDS)]
        d, dd = {}, {}
        bx, by = s[19] * (STEP / 12.0), s[20] * (STEP / 12.0)
        partial = {}
        for f in FIRST + tuple(f for f in range(FIELDS) if f not in FIRST):
            c = s[f]
            half, slot = divmod(f, 16)
            ghost = pltpu.roll(ghosts[half], (128 - 8 * slot - 3) % 128, 1)
            up = [pad[f, z + 3, pl.ds(row + 8 + k, 8), :] for k in (1, 2, 3)]
            down = [pad[f, z + 3, pl.ds(row + 8 - k, 8), :] for k in (1, 2, 3)]
            right_ = [pltpu.roll(jnp.where(lane < k, ghost, c), 128 - k, 1) for k in (1, 2, 3)]
            left_ = [pltpu.roll(jnp.where(lane >= 128 - k, ghost, c), k, 1) for k in (1, 2, 3)]
            dx = 8.0 * (up[0] - down[0]) - (up[1] - down[1])
            dy = 8.0 * (right_[0] - left_[0]) - (right_[1] - left_[1])
            sx = [up[k] + down[k] for k in range(3)]
            sy = [right_[k] + left_[k] for k in range(3)]
            smooth = (sx[2] + sy[2]) - 6.0 * (sx[1] + sy[1]) + 15.0 * (sx[0] + sy[0]) - 40.0 * c
            partial[f] = bx * dx + by * dy + damp * smooth
            if f in FIRST:
                zs = {k: pad[f, z + 3 + k, pl.ds(row + 8, 8), :] for k in (-2, -1, 1, 2)}
                dz = 8.0 * (zs[1] - zs[-1]) - (zs[2] - zs[-2])
                sz = [zs[1] + zs[-1], zs[2] + zs[-2]]
                d[f] = [v * (1.0 / 12.0) for v in (dx, dy, dz)]
                dd[f] = [(16.0 * v[0] - v[1] - 30.0 * c) * (1.0 / 12.0) for v in (sx, sy, sz)]
        rhs = evolve(s, d, dd)
        for f in range(FIELDS):
            at = (f, z, pl.ds(row, 8), slice(None))
            acc[at] = acc[at] + (partial[f] + STEP * rhs[f])

    @pl.loop(0, 2 * ROWS_Z)
    def _(i):
        tile(i // 2, pl.multiple_of(8 + 8 * (i % 2), 8))

    @pl.when(z > 0)
    def _():
        to_up.wait_recv()

    @pl.when(z < 7)
    def _():
        to_down.wait_recv()

    @pl.when(is_first)
    def _():
        for q in range(8):
            piece(0, q).wait_recv()

    @pl.when(is_last)
    def _():
        for q in range(8):
            piece(1, q).wait_recv()

    @pl.when(gx == 0)
    def _():
        for copy in to_mirror:
            copy.wait_recv()
        turn = jnp.where(
            lax.broadcasted_iota(jnp.int32, (128, 128), 0) + lax.broadcasted_iota(jnp.int32, (128, 128), 1) == 127,
            1.0, 0.0,
        )

        @pl.loop(0, FIELDS)
        def _(f):
            sign = (1 - 2 * ((NEGATIVE_BITS >> f) & 1)).astype(jnp.float32)
            rows = pad[f, 3:11, 0:8, :].reshape(64, 128)
            rows = jnp.dot(rows, turn, precision=lax.Precision.HIGHEST, preferred_element_type=jnp.float32)
            pad[f, 3:11, 0:8, :] = (rows * sign).reshape(8, 8, 128)

    @pl.when(gx == 15)
    def _():
        @pl.loop(0, FIELDS)
        def _(f):
            edge = pad[f, 3:11, 39:40, :]
            pad[f, 3:11, 40:43, :] = jnp.broadcast_to(edge, (8, 3, 128))

    @pl.loop(0, 2 * ROWS_Z)
    def _(i):
        tile(i // 2, pl.multiple_of(24 * (i % 2), 8))

    @pl.when(z > 0)
    def _():
        to_down.wait_send()

    @pl.when(z < 7)
    def _():
        to_up.wait_send()

    @pl.when(gx == 0)
    def _():
        for copy in to_mirror:
            copy.wait_send()

    @pl.when(is_last)
    def _():
        for q in range(8):
            leg_out(0, q).wait_send()

    @pl.when(is_first)
    def _():
        for q in range(8):
            leg_out(1, q).wait_send()

    @pl.when((gx != 7) & (gx != 8))
    def _():
        piece(0, 0).wait_send()

    @pl.when(gy > 0)
    def _():
        to_left.wait_send()

    @pl.when(gy < 7)
    def _():
        to_right.wait_send()

    def along_z(f):
        for row in range(0, ROWS_X, 8):
            v = [pad[f, z, pl.ds(row + 8, 8), :] for z in range(14)]
            for z in range(8):
                w = v[z:z + 7]
                bz = pad[21, z + 3, pl.ds(row + 8, 8), :] * (STEP / 12.0)
                dz = 8.0 * (w[4] - w[2]) - (w[5] - w[1])
                smooth = (w[6] + w[0]) - 6.0 * (w[5] + w[1]) + 15.0 * (w[4] + w[2]) - 20.0 * w[3]
                at = (f, z, pl.ds(row, 8), slice(None))
                acc[at] = acc[at] + (bz * dz + damp * smooth)

    @pl.loop(0, FIELDS)
    def _(n):
        @pl.when(n >= len(FIRST))
        def _():
            for copy in z_copies(n):
                copy.wait_recv()

        along_z(field_at(n))
        for copy in z_copies(n):
            copy.wait_send()


def body(section_fields, base_fields, flags):
    f32 = jnp.float32
    block = (FIELDS, ROWS_Z, ROWS_X, ROWS_Y)
    dma = pltpu.SemaphoreType.DMA
    return pl.pallas_call(
        kernel,
        out_shape=jax.ShapeDtypeStruct(block, f32),
        in_specs=[
            pl.BlockSpec(memory_space=pl.ANY),
            pl.BlockSpec(memory_space=pl.ANY),
            pl.BlockSpec(memory_space=pl.ANY),
        ],
        out_specs=pl.BlockSpec(memory_space=pltpu.VMEM),
        scratch_shapes=[
            pltpu.VMEM((FIELDS, 14, 48, ROWS_Y), f32),
            pltpu.VMEM((FIELDS, 8, ROWS_Y), f32),
            pltpu.VMEM((2, ROWS_Z, ROWS_X, ROWS_Y), f32),
            pltpu.VMEM((2, ROWS_Z, ROWS_X, ROWS_Y), f32),
            pltpu.VMEM((2, ROWS_Z, ROWS_X, ROWS_Y), f32),
            pltpu.SMEM((1, 1), jnp.int32),
            dma((3,)),
            dma((2, FIELDS)),
            dma((2, FIELDS)),
            dma((5,)),
            dma((5,)),
            dma((2,)),
            dma((2,)),
            dma((9,)),
            dma((1,)),
            dma((8,)),
            pltpu.SemaphoreType.REGULAR((6,)),
        ],
        compiler_params=pltpu.CompilerParams(
            collective_id=0, has_side_effects=True, vmem_limit_bytes=48 * 2**20
        ),
        cost_estimate=pl.CostEstimate(flops=80_000_000, bytes_accessed=9_830_400, transcendentals=0),
        name="substep",
    )(section_fields, base_fields, flags)


def solution(mesh):
    spec = P(None, "gz", "gx", "gy")
    return jax.shard_map(
        body, mesh=mesh, in_specs=(spec, spec, P("gx", "gy")), out_specs=spec, check_vma=False
    )
```

```python
import jax
import jax.numpy as jnp
from jax import lax
from jax.experimental import pallas as pl
from jax.experimental.pallas import tpu as pltpu
from jax.sharding import PartitionSpec as P

MESH = pl.DeviceIdType.MESH
FIELDS = 25
PAIRS = ((0, 0), (0, 1), (0, 2), (1, 1), (1, 2), (2, 2))
NEGATIVE = (3, 5, 10, 12, 14, 15, 19, 20, 22, 23)
NEGATIVE_BITS = sum(1 << c for c in NEGATIVE)
FIRST = (17, 19, 20, 21)
EARLY = 8
NEAR = 2
ROWS_Z, ROWS_X, ROWS_Y = 8, 32, 128
TILES = ROWS_X // 8
STEP = 0.25


def field_at(n):
    rest = jnp.where(n < 21, n - 4, jnp.where(n < 22, 18, n))
    return jnp.where(n < 1, 17, jnp.where(n < 4, 18 + n, rest))


def remote(src, dst, send, recv, device):
    return pltpu.make_async_remote_copy(
        src_ref=src, dst_ref=dst, send_sem=send, recv_sem=recv, device_id=device, device_id_type=MESH
    )


def sym(i, j):
    return PAIRS.index((min(i, j), max(i, j)))


def evolve(s, d, dd):
    chi, trace, lapse, theta = s[0], s[7], s[17], s[18]
    g = lambda i, j: s[1 + sym(i, j)]
    a = lambda i, j: s[8 + sym(i, j)]
    grad = lambda k, j: d[19 + k][j]
    div = grad(0, 0) + grad(1, 1) + grad(2, 2)
    lap = dd[17][0] + dd[17][1] + dd[17][2]
    div23 = (2.0 / 3.0) * div
    square = (
        a(0, 0) * a(0, 0) + a(1, 1) * a(1, 1) + a(2, 2) * a(2, 2)
        + 2.0 * (a(0, 1) * a(0, 1) + a(0, 2) * a(0, 2) + a(1, 2) * a(1, 2))
    )
    out = {}
    out[0] = chi * ((2.0 / 3.0) * (lapse * trace) - div23)
    lapse2 = 2.0 * lapse
    for n, (i, j) in enumerate(PAIRS):
        if i == j:
            lie_g = 2.0 * sum(g(i, k) * grad(k, i) for k in range(3))
            lie_a = 2.0 * sum(a(i, k) * grad(k, i) for k in range(3))
        else:
            lie_g = sum(g(i, k) * grad(k, j) + g(j, k) * grad(k, i) for k in range(3))
            lie_a = sum(a(i, k) * grad(k, j) + a(j, k) * grad(k, i) for k in range(3))
        out[1 + n] = lie_g - lapse2 * a(i, j) - g(i, j) * div23
        quad = sum(a(i, k) * a(k, j) for k in range(3))
        term = lapse * (trace * a(i, j)) - lapse2 * quad + lie_a - a(i, j) * div23
        if i == j:
            term = term + chi * (lap * (1.0 / 3.0) - dd[17][i])
        out[8 + n] = term
    third = trace * trace * (1.0 / 3.0)
    out[7] = lapse * (square + third) - chi * lap
    for i in range(3):
        value = dd[19 + i][0] + dd[19 + i][1] + dd[19 + i][2]
        value = value - 2.0 * sum(a(i, j) * d[17][j] for j in range(3))
        value = value + s[14 + i] * div23
        value = value - sum(s[14 + j] * grad(i, j) for j in range(3))
        out[14 + i] = value
        out[22 + i] = value - 2.0 * s[22 + i]
        out[19 + i] = 0.75 * s[22 + i]
    out[17] = -lapse2 * (trace - 2.0 * theta)
    out[18] = lapse * (third - 0.5 * square) - 0.04 * (lapse * theta)
    return out


def kernel(
    sec, base, flag, acc,
    pad, cross, packed, from_left, from_right, flag_at,
    load_sem, z_send, z_recv, x_send, x_recv, y_send, y_recv, leg_send, leg_recv, arrive_recv, hello,
):
    gx, gy, gz = lax.axis_index("gx"), lax.axis_index("gy"), lax.axis_index("gz")
    low, z, core = gx // 8, gx % 8, gy % 2
    partner = (gx, gy, 1 - gz)
    left, right = (gx, (gy + 7) % 8, gz), (gx, (gy + 1) % 8, gz)
    up, down = (gx + 1, gy, gz), (gx - 1, gy, gz)
    mirror = (0, 7 - gy, gz)
    last, first = (7, gy, gz), (8, gy, gz)
    is_last, is_first = gx == 7, gx == 8
    in_row = lambda half, q: (8 * half + q, gy, gz)

    load_s = pltpu.make_async_copy(sec, pad.at[:, 3:11, 8:40, :], load_sem.at[0])
    load_b = pltpu.make_async_copy(base, acc, load_sem.at[1])
    load_f = pltpu.make_async_copy(flag, flag_at, load_sem.at[2])
    barrier = pltpu.get_barrier_semaphore()

    def tell(semaphore, device):
        pl.semaphore_signal(semaphore, inc=1, device_id=device, device_id_type=MESH)

    tell(barrier, partner)
    load_f.start()

    @pl.when(core == 1)
    def _():
        tell(barrier, left)
        tell(barrier, right)

    @pl.when((core == 1) & (gx == 0))
    def _():
        tell(barrier, mirror)

    @pl.when(z < 4)
    def _():
        tell(barrier, up)

    @pl.when(z == 0)
    def _():
        for q in range(4, 8):
            tell(barrier, (gx + q, gy, gz))

    @pl.when(z < NEAR)
    def _():
        tell(barrier, last)

    @pl.when(gx == 0)
    def _():
        tell(barrier, first)

    @pl.when(is_first)
    def _():
        for q in range(8):
            if q > 0:
                tell(barrier, in_row(0, q))
                tell(barrier, in_row(1, q))

    expected = (
        1 + jnp.where(core == 0, 2, 0) + jnp.where((core == 0) & (gx == 0), 1, 0) + jnp.where(z > 0, 1, 0) + jnp.where(z == 4, 1, 0)
        + jnp.where(is_last, 2 * NEAR, 0) + jnp.where(gx == 0, 0, 1)
    )
    pl.semaphore_wait(barrier, expected)

    def z_copies(n):
        f = field_at(n)
        return (
            remote(sec.at[f, 0:3], pad.at[f, 11:14, 8:40, :], z_send.at[0, n], z_recv.at[0, n], partner),
            remote(sec.at[f, 5:8], pad.at[f, 0:3, 8:40, :], z_send.at[1, n], z_recv.at[1, n], partner),
        )

    @pl.loop(0, EARLY)
    def _(n):
        for copy in z_copies(n):
            copy.start()

    def start_rest():
        @pl.loop(EARLY, FIELDS)
        def _(n):
            for copy in z_copies(n):
                copy.start()

    @pl.when((gx != 7) & (gx != 8))
    def _():
        start_rest()

    load_s.start()

    @pl.when((z > 0) & (z < 5))
    def _():
        tell(hello.at[0], down)

    @pl.when(z > 3)
    def _():
        tell(hello.at[0], (gx - z, gy, gz))

    @pl.when(core == 0)
    def _():
        tell(hello.at[1], left)
        tell(hello.at[1], right)

    @pl.when((core == 0) & (gx == 0))
    def _():
        tell(hello.at[2], mirror)

    @pl.when(((low == 0) & (z > 0)) | (z >= NEAR))
    def _():
        tell(hello.at[3], first)

    @pl.when(is_last)
    def _():
        for q in range(NEAR):
            tell(hello.at[4], in_row(0, q))
        tell(hello.at[5], first)

    to_up = remote(sec.at[:, :, 29:32, :], pad.at[:, 3:11, 5:8, :], x_send.at[3], x_recv.at[3], up)
    to_down = remote(sec.at[:, :, 0:3, :], pad.at[:, 3:11, 40:43, :], x_send.at[4], x_recv.at[4], down)
    to_mirror = [
        remote(sec.at[:, :, i:i + 1, :], pad.at[:, 3:11, 7 - i:8 - i, :], x_send.at[i], x_recv.at[i], mirror)
        for i in range(3)
    ]

    def leg_out(half, q):
        rows = slice(29, 32) if half == 0 else slice(0, 3)
        own = q == 7 * half
        ghost = piece_ghost(half, q) if own else cross.at[:, 0:3, :]
        return remote(
            sec.at[:, q, rows, :], ghost, leg_send.at[q], arrive_recv.at[q] if own else leg_recv.at[0], in_row(1 - half, q)
        )

    def piece_ghost(half, q):
        return pad.at[:, 3 + q, 5:8, :] if half == 0 else pad.at[:, 3 + q, 40:43, :]

    def leg_in(half):
        return remote(
            cross.at[:, 0:3, :], piece_ghost(half, z), leg_send.at[8], arrive_recv.at[z], first if half == 0 else last
        )

    def piece(half, q):
        return remote(cross.at[:, 0:3, :], piece_ghost(half, q), leg_send.at[8], arrive_recv.at[q], first)

    @pl.when((z > 0) & (z < 5))
    def _():
        to_down.start()

    @pl.when(is_last)
    def _():
        for q in range(NEAR):
            leg_out(0, q).start()

    lane = lax.broadcasted_iota(jnp.int32, (8, 128), 1)
    load_s.wait()

    @pl.loop(0, ROWS_Z * TILES)
    def _(i):
        z, row = i // TILES, pl.multiple_of((i % TILES) * 8, 8)
        both = [jnp.zeros((8, 128), jnp.float32) for _ in range(2)]
        for f in range(FIELDS):
            half, slot = divmod(f, 16)
            tile = pltpu.roll(pad[f, z + 3, pl.ds(row + 8, 8), :], 3 + 8 * slot, 1)
            both[half] = jnp.where(lane >= 8 * slot, tile, both[half])
        for half in range(2):
            packed[half, z, pl.ds(row, 8), :] = both[half]

    to_left = remote(packed, from_right, y_send.at[0], y_recv.at[0], left)
    to_right = remote(packed, from_left, y_send.at[1], y_recv.at[1], right)

    @pl.when(core == 1)
    def _():
        pl.semaphore_wait(hello.at[1], 2)

    @pl.when(gy > 0)
    def _():
        to_left.start()

    @pl.when(gy < 7)
    def _():
        to_right.start()

    @pl.when(z == 0)
    def _():
        pl.semaphore_wait(hello.at[0], 5)
        for q in range(4, 8):
            tell(hello.at[0], (gx + q, gy, gz))

    @pl.when(z > 0)
    def _():
        pl.semaphore_wait(hello.at[0], 1)

    @pl.when(z < 7)
    def _():
        to_up.start()

    @pl.when(z > 4)
    def _():
        to_down.start()

    @pl.when((core == 1) & (gx == 0))
    def _():
        pl.semaphore_wait(hello.at[2], 1)

    @pl.when(gx == 0)
    def _():
        for copy in to_mirror:
            copy.start()

    @pl.when(is_first)
    def _():
        pl.semaphore_wait(hello.at[3], 15 - NEAR)
        for q in range(8):
            leg_out(1, q).start()
        pl.semaphore_wait(hello.at[5], 1)
        for q in range(NEAR, 8):
            tell(hello.at[4], in_row(1, q))
        start_rest()

    @pl.when((low == 1) & (z >= NEAR))
    def _():
        pl.semaphore_wait(hello.at[4], 1)
        tell(hello.at[5], last)

    @pl.when(is_last)
    def _():
        pl.semaphore_wait(hello.at[5], 8 - NEAR)
        for q in range(NEAR, 8):
            leg_out(0, q).start()
        start_rest()

    @pl.when(gx < 6)
    def _():
        pl.semaphore_wait(hello.at[4], 1)

    @pl.when((gx > NEAR) & (gx < 7))
    def _():
        tell(hello.at[4], down)

    @pl.when(gx < 7)
    def _():
        leg_out(1, 0).wait_recv()
        leg_in(1).start()

    @pl.when(gx > 8)
    def _():
        leg_out(0, 1).wait_recv()
        leg_in(0).start()

    load_b.start()

    place = lax.broadcasted_iota(jnp.int32, (ROWS_X, 128), 1) % 8

    @pl.when(gy > 0)
    def _():
        to_right.wait_recv()

    @pl.when(gy < 7)
    def _():
        to_left.wait_recv()

    @pl.when(gy == 0)
    def _():
        @pl.loop(0, 2 * ROWS_Z)
        def _(i):
            own = packed[i // ROWS_Z, i % ROWS_Z]
            from_left[i // ROWS_Z, i % ROWS_Z] = jnp.where(
                place == 0, pltpu.roll(own, 125, 1),
                jnp.where(place == 1, pltpu.roll(own, 126, 1), pltpu.roll(own, 127, 1)),
            )

    @pl.when(gy == 7)
    def _():
        @pl.loop(0, 2 * ROWS_Z)
        def _(i):
            own = packed[i // ROWS_Z, i % ROWS_Z]
            from_right[i // ROWS_Z, i % ROWS_Z] = jnp.where(
                place == 3, pltpu.roll(own, 1, 1),
                jnp.where(place == 4, pltpu.roll(own, 2, 1), pltpu.roll(own, 3, 1)),
            )

    load_b.wait()
    load_f.wait()
    for n in range(len(FIRST)):
        for copy in z_copies(n):
            copy.wait_recv()

    sigma = 0.05 + 0.75 * flag_at[0, 0].astype(jnp.float32)
    damp = sigma * (STEP / 64.0)

    def tile(z, row):
        here = (z + 3, pl.ds(row + 8, 8), slice(None))
        ghosts = [
            jnp.where(lane % 8 < 3, from_left[half, z, pl.ds(row, 8), :], from_right[half, z, pl.ds(row, 8), :])
            for half in range(2)
        ]
        s = [pad[(f,) + here] for f in range(FIELDS)]
        d, dd = {}, {}
        bx, by = s[19] * (STEP / 12.0), s[20] * (STEP / 12.0)
        partial = {}
        for f in FIRST + tuple(f for f in range(FIELDS) if f not in FIRST):
            c = s[f]
            half, slot = divmod(f, 16)
            ghost = pltpu.roll(ghosts[half], (128 - 8 * slot - 3) % 128, 1)
            up = [pad[f, z + 3, pl.ds(row + 8 + k, 8), :] for k in (1, 2, 3)]
            down = [pad[f, z + 3, pl.ds(row + 8 - k, 8), :] for k in (1, 2, 3)]
            right_ = [pltpu.roll(jnp.where(lane < k, ghost, c), 128 - k, 1) for k in (1, 2, 3)]
            left_ = [pltpu.roll(jnp.where(lane >= 128 - k, ghost, c), k, 1) for k in (1, 2, 3)]
            dx = 8.0 * (up[0] - down[0]) - (up[1] - down[1])
            dy = 8.0 * (right_[0] - left_[0]) - (right_[1] - left_[1])
            sx = [up[k] + down[k] for k in range(3)]
            sy = [right_[k] + left_[k] for k in range(3)]
            smooth = (sx[2] + sy[2]) - 6.0 * (sx[1] + sy[1]) + 15.0 * (sx[0] + sy[0]) - 40.0 * c
            partial[f] = bx * dx + by * dy + damp * smooth
            if f in FIRST:
                zs = {k: pad[f, z + 3 + k, pl.ds(row + 8, 8), :] for k in (-2, -1, 1, 2)}
                dz = 8.0 * (zs[1] - zs[-1]) - (zs[2] - zs[-2])
                sz = [zs[1] + zs[-1], zs[2] + zs[-2]]
                d[f] = [v * (1.0 / 12.0) for v in (dx, dy, dz)]
                dd[f] = [(16.0 * v[0] - v[1] - 30.0 * c) * (1.0 / 12.0) for v in (sx, sy, sz)]
        rhs = evolve(s, d, dd)
        for f in range(FIELDS):
            at = (f, z, pl.ds(row, 8), slice(None))
            acc[at] = acc[at] + (partial[f] + STEP * rhs[f])

    @pl.loop(0, 2 * ROWS_Z)
    def _(i):
        tile(i // 2, pl.multiple_of(8 + 8 * (i % 2), 8))

    @pl.when(z > 0)
    def _():
        to_up.wait_recv()

    @pl.when(z < 7)
    def _():
        to_down.wait_recv()

    @pl.when(is_first)
    def _():
        for q in range(8):
            piece(0, q).wait_recv()

    @pl.when(is_last)
    def _():
        for q in range(8):
            piece(1, q).wait_recv()

    @pl.when(gx == 0)
    def _():
        for copy in to_mirror:
            copy.wait_recv()
        turn = jnp.where(
            lax.broadcasted_iota(jnp.int32, (128, 128), 0) + lax.broadcasted_iota(jnp.int32, (128, 128), 1) == 127,
            1.0, 0.0,
        )

        @pl.loop(0, FIELDS)
        def _(f):
            sign = (1 - 2 * ((NEGATIVE_BITS >> f) & 1)).astype(jnp.float32)
            rows = pad[f, 3:11, 0:8, :].reshape(64, 128)
            rows = jnp.dot(rows, turn, precision=lax.Precision.HIGHEST, preferred_element_type=jnp.float32)
            pad[f, 3:11, 0:8, :] = (rows * sign).reshape(8, 8, 128)

    @pl.when(gx == 15)
    def _():
        @pl.loop(0, FIELDS)
        def _(f):
            edge = pad[f, 3:11, 39:40, :]
            pad[f, 3:11, 40:43, :] = jnp.broadcast_to(edge, (8, 3, 128))

    @pl.loop(0, 2 * ROWS_Z)
    def _(i):
        tile(i // 2, pl.multiple_of(24 * (i % 2), 8))

    @pl.when(z > 0)
    def _():
        to_down.wait_send()

    @pl.when(z < 7)
    def _():
        to_up.wait_send()

    @pl.when(gx == 0)
    def _():
        for copy in to_mirror:
            copy.wait_send()

    @pl.when(is_last)
    def _():
        for q in range(8):
            leg_out(0, q).wait_send()

    @pl.when(is_first)
    def _():
        for q in range(8):
            leg_out(1, q).wait_send()

    @pl.when((gx != 7) & (gx != 8))
    def _():
        piece(0, 0).wait_send()

    @pl.when(gy > 0)
    def _():
        to_left.wait_send()

    @pl.when(gy < 7)
    def _():
        to_right.wait_send()

    @pl.loop(0, FIELDS)
    def _(f):
        for row in range(0, ROWS_X, 8):
            own = [pad[f, z, pl.ds(row + 8, 8), :] for z in range(3, 11)]
            none = [jnp.zeros((8, 128), jnp.float32)] * 3
            v = none + own + none
            for z in range(8):
                w = v[z:z + 7]
                bz = pad[21, z + 3, pl.ds(row + 8, 8), :] * (STEP / 12.0)
                dz = 8.0 * (w[4] - w[2]) - (w[5] - w[1])
                smooth = (w[6] + w[0]) - 6.0 * (w[5] + w[1]) + 15.0 * (w[4] + w[2]) - 20.0 * w[3]
                at = (f, z, pl.ds(row, 8), slice(None))
                acc[at] = acc[at] + (bz * dz + damp * smooth)

    def along_z(f):
        for row in range(0, ROWS_X, 8):
            for side, edge in ((-1, 0), (1, 7)):
                g = [pad[f, edge + 3 + side * k, pl.ds(row + 8, 8), :] for k in (1, 2, 3)]
                b = [pad[21, edge + 3 - side * k, pl.ds(row + 8, 8), :] * (side * STEP / 12.0) for k in (0, 1)]
                parts = (
                    b[0] * (8.0 * g[0] - g[1]) + damp * (g[2] - 6.0 * g[1] + 15.0 * g[0]),
                    damp * (g[1] - 6.0 * g[0]) - b[1] * g[0],
                    damp * g[0],
                )
                for k, part in enumerate(parts):
                    at = (f, edge - side * k, pl.ds(row, 8), slice(None))
                    acc[at] = acc[at] + part

    @pl.loop(0, FIELDS)
    def _(n):
        @pl.when(n >= len(FIRST))
        def _():
            for copy in z_copies(n):
                copy.wait_recv()

        along_z(field_at(n))
        for copy in z_copies(n):
            copy.wait_send()


def body(section_fields, base_fields, flags):
    f32 = jnp.float32
    block = (FIELDS, ROWS_Z, ROWS_X, ROWS_Y)
    dma = pltpu.SemaphoreType.DMA
    return pl.pallas_call(
        kernel,
        out_shape=jax.ShapeDtypeStruct(block, f32),
        in_specs=[
            pl.BlockSpec(memory_space=pl.ANY),
            pl.BlockSpec(memory_space=pl.ANY),
            pl.BlockSpec(memory_space=pl.ANY),
        ],
        out_specs=pl.BlockSpec(memory_space=pltpu.VMEM),
        scratch_shapes=[
            pltpu.VMEM((FIELDS, 14, 48, ROWS_Y), f32),
            pltpu.VMEM((FIELDS, 8, ROWS_Y), f32),
            pltpu.VMEM((2, ROWS_Z, ROWS_X, ROWS_Y), f32),
            pltpu.VMEM((2, ROWS_Z, ROWS_X, ROWS_Y), f32),
            pltpu.VMEM((2, ROWS_Z, ROWS_X, ROWS_Y), f32),
            pltpu.SMEM((1, 1), jnp.int32),
            dma((3,)),
            dma((2, FIELDS)),
            dma((2, FIELDS)),
            dma((5,)),
            dma((5,)),
            dma((2,)),
            dma((2,)),
            dma((9,)),
            dma((1,)),
            dma((8,)),
            pltpu.SemaphoreType.REGULAR((6,)),
        ],
        compiler_params=pltpu.CompilerParams(
            collective_id=0, has_side_effects=True, vmem_limit_bytes=48 * 2**20
        ),
        cost_estimate=pl.CostEstimate(flops=80_000_000, bytes_accessed=9_830_400, transcendentals=0),
        name="substep",
    )(section_fields, base_fields, flags)


def solution(mesh):
    spec = P(None, "gz", "gx", "gy")
    return jax.shard_map(
        body, mesh=mesh, in_specs=(spec, spec, P("gx", "gy")), out_specs=spec, check_vma=False
    )
```
